1024 devices in a mesh: group: 8 (over y), expert: 64 (over x, z), ffn: 2 (over core).
Axes of the slice: x: 4, y: 8, z: 16, core: 2. Of those that a mesh axis runs over, the one named last changes fastest.
Arguments:
- tokens: bfloat16 [2048, 3584], P(('group', 'expert')), may hold values from -6 to 6
- cotangent: bfloat16 [2048, 3584], P(('group', 'expert')), may hold values from -6 to 6
- group_ids: int32 [2048, 4], P(('group', 'expert')), may hold values from 0 to 7, as said below
- expert_ids: int32 [2048, 8], P(('group', 'expert')), may hold values from 0 to 15, as said below
- gate_weights: bfloat16 [2048, 8], P(('group', 'expert')), may hold values from 0.049804688 to 0.5
- w_gate: bfloat16 [512, 3584, 256], P(('group', 'expert'), None, 'ffn'), may hold values from -0.09375 to 0.09375
- w_up: bfloat16 [512, 3584, 256], P(('group', 'expert'), None, 'ffn'), may hold values from -0.09375 to 0.09375
- w_down: bfloat16 [512, 256, 3584], P(('group', 'expert'), 'ffn'), may hold values from -0.1875 to 0.1875
Outputs:
- mixed: bfloat16 [2048, 3584], P(('group', 'expert'), 'ffn')
- token_grad: bfloat16 [2048, 3584], P(('group', 'expert'), 'ffn')
- gate_grad: float32 [2048, 8], P(('group', 'expert'), 'ffn')
The draws below stay inside these ranges and needn't reach their ends.
Inputs may be any that keep to these rules, and one draw needn't show every extreme that they name: `group_ids`: each row names 4 different groups. `expert_ids`: entries 2 j and 2 j + 1 of a row are two different experts of group group_ids[t, j].
All inputs are finite; a program needn't handle non-finite values.
Results may differ from the reference program's by a relative error of at most 0.025.
Values may be sent and summed in bfloat16 or wider, within the bound.
A program may use at most 32 MiB of HBM per device.

```python
import jax
import jax.numpy as jnp
from jax import lax

D = 3584
FF = 1024
EXPERTS = 128
TOPG = 4
TOPK = 8
CAP = 2
TOK_DEV = 4
TOKENS = 2048
GROUP_EXPERTS = 16
SUBSLICES = 4
SLICE_UNITS = 256
DEV_UNITS = 128
N_GROUP = 8
N_EXPERT = 64
N_FFN = 2


def draw_group_ids(key, part):
    key = jax.random.fold_in(key, 11)
    scores = jax.random.randint(key, (TOKENS, N_GROUP), 0, 1 << 20) * N_GROUP + jnp.arange(N_GROUP)[None, :]
    ranked = jnp.argsort(scores, axis=1, stable=True)
    return ranked[:, :TOPG].astype(jnp.int32)


def draw_expert_ids(key, part):
    key = jax.random.fold_in(key, 23)
    key_hot, key_coin, key_index, key_drawn, key_offset = jax.random.split(key, 5)
    hot_experts = jax.random.permutation(key_hot, GROUP_EXPERTS)[:4].astype(jnp.int32)
    coin_flip = jax.random.randint(key_coin, (TOKENS, TOPG), 0, 2)
    hot_index = jax.random.randint(key_index, (TOKENS, TOPG), 0, 4)
    drawn_pick = jax.random.randint(key_drawn, (TOKENS, TOPG), 0, GROUP_EXPERTS)
    first_pick = jnp.where(coin_flip == 1, hot_experts[hot_index], drawn_pick)
    offset_pick = jax.random.randint(key_offset, (TOKENS, TOPG), 0, GROUP_EXPERTS - 1)
    second = (first_pick + 1 + offset_pick) % GROUP_EXPERTS
    return jnp.stack([first_pick, second], axis=2).reshape(TOKENS, TOPK).astype(jnp.int32)


def level_of(rng, shape, shards, smallest, top_value):
    def one(dim, parts):
        draws = jax.random.uniform(jax.random.fold_in(jax.random.fold_in(rng, 6), dim), (parts,), jnp.float32, smallest / len(shards), top_value / len(shards))
        return jnp.repeat(jnp.exp(draws), shape[dim] // parts).reshape((-1,) + (1,) * (len(shape) - dim - 1))

    factor_of = one(*shards[0])
    for cut in shards[1:]:
        factor_of = factor_of * one(*cut)
    return factor_of


def noise(rng, shape, scale, most, cuts=(), kind=jnp.bfloat16):
    result = jax.random.normal(rng, shape, jnp.float32) * scale
    if len(cuts) > 0:
        result = level_of(rng, shape, cuts, -0.22, 0.18) * result
    return jnp.clip(result, min=-most, max=most).astype(kind)


def setup_inputs(seed: int = 0) -> dict:
    streams_of = jax.random.split(jax.random.key(seed), 9)
    return {
        "tokens": noise(streams_of[0], (TOKENS, D), 1.0, 6.0, ((0, 512),)),
        "cotangent": noise(streams_of[1], (TOKENS, D), 1.0, 6.0, ((0, 512),)),
        "group_ids": draw_group_ids(jax.random.fold_in(streams_of[8], 71), 0),
        "expert_ids": draw_expert_ids(jax.random.fold_in(streams_of[8], 71), 0),
        "gate_weights": jnp.clip(0.049804688 + 0.4501953 * jax.random.uniform(streams_of[4], (TOKENS, TOPK), jnp.float32) ** level_of(streams_of[4], (TOKENS, TOPK), ((0, 512),), -0.2, 0.2), 0.049804688, 0.5).astype(jnp.bfloat16),
        "w_gate": noise(streams_of[5], (EXPERTS * SUBSLICES, D, SLICE_UNITS), D ** -0.5, 0.09375, ((0, 512), (2, 2))),
        "w_up": noise(streams_of[6], (EXPERTS * SUBSLICES, D, SLICE_UNITS), D ** -0.5, 0.09375, ((0, 512), (2, 2))),
        "w_down": noise(streams_of[7], (EXPERTS * SUBSLICES, SLICE_UNITS, D), FF ** -0.5, 0.1875, ((0, 512), (1, 2))),
    }


def expert_slice(slot_rows, slot_grads, gate_part, up_part, down_part):
    gate_pre = jnp.dot(slot_rows, gate_part, preferred_element_type=jnp.float32)
    up_pre = jnp.dot(slot_rows, up_part, preferred_element_type=jnp.float32)
    sigmoid_gate = jax.nn.sigmoid(gate_pre)
    active = gate_pre * sigmoid_gate
    hidden = (active * up_pre).astype(jnp.bfloat16)
    part_out = jnp.dot(hidden, down_part, preferred_element_type=jnp.float32).astype(jnp.bfloat16)
    back_hidden = jnp.dot(slot_grads, down_part.T, preferred_element_type=jnp.float32)
    gate_back = (back_hidden * up_pre * sigmoid_gate * (1.0 + gate_pre * (1.0 - sigmoid_gate))).astype(jnp.bfloat16)
    up_back = (back_hidden * active).astype(jnp.bfloat16)
    part_in = (jnp.dot(gate_back, gate_part.T, preferred_element_type=jnp.float32)
               + jnp.dot(up_back, up_part.T, preferred_element_type=jnp.float32)).astype(jnp.bfloat16)
    part_score = jnp.sum(slot_grads.astype(jnp.float32) * part_out.astype(jnp.float32), axis=1).astype(jnp.bfloat16)
    return part_out, part_in, part_score


def reference(tokens, cotangent, group_ids, expert_ids, gate_weights, w_gate, w_up, w_down):
    pair_count = TOPK // TOPG
    pick_group = jnp.repeat(group_ids, pair_count, axis=1).astype(jnp.int32)
    pick_expert = (pick_group * GROUP_EXPERTS + expert_ids).astype(jnp.int32)
    counts = jnp.sum((pick_expert[:, :, None] == jnp.arange(EXPERTS, dtype=jnp.int32)[None, None, :]).astype(jnp.int32), axis=1).astype(jnp.int32)
    blocks = counts.reshape(N_GROUP, N_EXPERT, TOK_DEV, EXPERTS).transpose(1, 0, 2, 3).reshape(N_EXPERT, N_GROUP * TOK_DEV, EXPERTS)
    earlier = (jnp.cumsum(blocks, axis=1) - blocks).astype(jnp.int32)
    earlier = earlier.reshape(N_EXPERT, N_GROUP, TOK_DEV, EXPERTS).transpose(1, 0, 2, 3).reshape(TOKENS, EXPERTS)
    position = jnp.take_along_axis(earlier, pick_expert, axis=1).astype(jnp.int32)
    kept_mask = position < CAP
    token_index = jnp.arange(TOKENS, dtype=jnp.int32)
    column = (token_index // TOK_DEV) % N_EXPERT
    slot_total = N_EXPERT * CAP
    target = pick_expert * slot_total + column[:, None] * CAP + position
    target = jnp.where(kept_mask, target, EXPERTS * slot_total).astype(jnp.int32).reshape(-1)
    slot_token = jnp.zeros((EXPERTS * slot_total,), jnp.int32).at[target].set(jnp.repeat(token_index, TOPK), mode="drop")
    slot_pick = jnp.zeros((EXPERTS * slot_total,), jnp.int32).at[target].set(jnp.tile(jnp.arange(TOPK, dtype=jnp.int32), TOKENS), mode="drop")
    valid_mask = jnp.zeros((EXPERTS * slot_total,), jnp.float32).at[target].set(jnp.ones((TOKENS * TOPK,), jnp.float32), mode="drop")
    slot_weight = jnp.zeros((EXPERTS * slot_total,), jnp.float32).at[target].set(gate_weights.astype(jnp.float32).reshape(-1), mode="drop")

    def one_expert(totals, expert_id):
        mixed_acc, grad_acc, score_acc = totals
        begin_at = (expert_id * slot_total).astype(jnp.int32)
        tokens_here = lax.dynamic_slice_in_dim(slot_token, begin_at, slot_total)
        picks_here = lax.dynamic_slice_in_dim(slot_pick, begin_at, slot_total)
        live_slots = lax.dynamic_slice_in_dim(valid_mask, begin_at, slot_total)
        weights_here = lax.dynamic_slice_in_dim(slot_weight, begin_at, slot_total)
        slot_rows = jnp.take(tokens, tokens_here, axis=0)
        slot_grads = jnp.take(cotangent, tokens_here, axis=0)
        block_start = (expert_id * SUBSLICES).astype(jnp.int32)
        gate_block = lax.dynamic_slice_in_dim(w_gate, block_start, SUBSLICES, 0)
        up_block = lax.dynamic_slice_in_dim(w_up, block_start, SUBSLICES, 0)
        down_block = lax.dynamic_slice_in_dim(w_down, block_start, SUBSLICES, 0)
        out_total = jnp.zeros((slot_total, D), jnp.float32)
        in_total = jnp.zeros((slot_total, D), jnp.float32)
        score_total = jnp.zeros((slot_total,), jnp.float32)
        for sub_index in range(SUBSLICES):
            for ffn_slot in range(N_FFN):
                first_unit = ffn_slot * DEV_UNITS
                part_out, part_in, part_score = expert_slice(
                    slot_rows, slot_grads,
                    gate_block[sub_index, :, first_unit:first_unit + DEV_UNITS],
                    up_block[sub_index, :, first_unit:first_unit + DEV_UNITS],
                    down_block[sub_index, first_unit:first_unit + DEV_UNITS, :])
                out_total = out_total + part_out.astype(jnp.float32)
                in_total = in_total + part_in.astype(jnp.float32)
                score_total = score_total + part_score.astype(jnp.float32)
        factor = (live_slots * weights_here)[:, None]
        mixed_acc = mixed_acc.at[tokens_here].add(out_total * factor)
        grad_acc = grad_acc.at[tokens_here].add(in_total * factor)
        score_acc = score_acc.at[tokens_here, picks_here].add(score_total * live_slots)
        return (mixed_acc, grad_acc, score_acc), None

    start_totals = (jnp.zeros((TOKENS, D), jnp.float32), jnp.zeros((TOKENS, D), jnp.float32), jnp.zeros((TOKENS, TOPK), jnp.float32))
    totals, unused = lax.scan(one_expert, start_totals, jnp.arange(EXPERTS, dtype=jnp.int32))
    return totals[0].astype(jnp.bfloat16), totals[1].astype(jnp.bfloat16), totals[2]
```

```python
import functools

import jax
import jax.numpy as jnp
from jax import lax
from jax.experimental import pallas as pl
from jax.experimental.pallas import tpu as pltpu
from jax.sharding import PartitionSpec as P

CAP = 2
NZ = 16
MESH = pl.DeviceIdType.MESH
F32 = jnp.float32
BF16 = jnp.bfloat16


def iota(shape, dim):
    return lax.broadcasted_iota(jnp.int32, shape, dim)


def dot(a, b):
    return jnp.dot(a, b, preferred_element_type=F32)


def dot_nt(a, b):
    return lax.dot_general(a, b, (((1,), (1,)), ((), ())), preferred_element_type=F32)


def kernel(
    ny, nx, per_group,
    tok_ref, cot_ref, gid_ref, eid_ref, gw_ref, wg_hbm, wu_hbm, wd_hbm,
    mixed_ref, grad_ref, score_ref,
    wg, wu, wd, wdt, wgt, wut,
    msg32, gbuf, ibuf, packed, xbuf, mbuf, zbuf, obuf, pin, cbuf, in_left, in_right,
    fin, rp, ret, ymsg, ybuf, smsg, sbuf,
    wsem, gs, gr, isem, ir, xs, xr, zds, zr, zfr, zfl, cs, cr, ps, pr,
    los, lor, ros, ror, fs, fr, xbs, xbr, ys, yr, ss, sr,
):
    y = lax.axis_index("group")
    e = lax.axis_index("expert")
    c = lax.axis_index("ffn")
    x = e // NZ
    z = e % NZ
    q = z // 4
    r = z % 4
    other = 1 - c
    width = msg32.shape[1]
    top_k = eid_ref.shape[1]
    rows_m = mbuf.shape[1]
    half_m = rows_m // 2
    quart_m = rows_m // 4
    n_in = ny * 16
    n_out = nx * 32

    def dev(yy, xx, zz, cc):
        return (yy, xx * NZ + zz, cc)

    def remote(src, dst, send, recv, where):
        return pltpu.make_async_remote_copy(
            src_ref=src, dst_ref=dst, send_sem=send, recv_sem=recv,
            device_id=where, device_id_type=MESH,
        )

    weight_copies = [
        pltpu.make_async_copy(wg_hbm.at[0], wg, wsem.at[0]),
        pltpu.make_async_copy(wu_hbm.at[0], wu, wsem.at[1]),
        pltpu.make_async_copy(wd_hbm.at[0], wd, wsem.at[2]),
    ]
    for cp in weight_copies:
        cp.start()

    barrier = pltpu.get_barrier_semaphore()
    partners = [dev(y, x, z, other)]
    for d in range(1, ny):
        for cc in range(2):
            partners.append(dev((y + d) % ny, x, z, cc))
    for d in range(1, nx):
        partners.append(dev(y, (x + d) % nx, z, c))
    for d in range(1, NZ):
        partners.append(dev(y, x, (z + d) % NZ, c))
    for where in partners:
        pl.semaphore_signal(barrier, inc=1, device_id=where, device_id_type=MESH)

    for h in range(2):
        for a, ref in enumerate((tok_ref, cot_ref)):
            start = pl.multiple_of(c * (2 * width) + h * width, 128)
            msg32[h * 8 + a * 4:h * 8 + a * 4 + 4, :] = ref[:, pl.ds(start, width)].astype(F32)
    gbuf[y] = msg32[...].astype(BF16)
    lane4 = iota((4, 128), 1)
    gid = gid_ref[...].astype(F32)
    eid = eid_ref[...].astype(F32)
    gw = gw_ref[...].astype(F32)
    info = jnp.zeros((4, 128), F32)
    for k in range(top_k):
        ident = gid[:, k // 2:k // 2 + 1] * float(per_group) + eid[:, k:k + 1]
        info = jnp.where(lane4 == k, ident, info)
        info = jnp.where(lane4 == top_k + k, gw[:, k:k + 1], info)
    ibuf[y] = jnp.full((8, 128), -1.0, F32)
    ibuf[y, 0:4, :] = info

    pl.semaphore_wait(barrier, len(partners))

    sends = []
    for d in range(1, ny):
        where = dev((y + d) % ny, x, z, c)
        sends.append(remote(ibuf.at[y], ibuf.at[y], isem.at[d], ir.at[d], where))
        sends[-1].start()
    for d in range(1, ny):
        where = dev((y + d) % ny, x, z, c)
        sends.append(remote(gbuf.at[y], gbuf.at[y], gs.at[d], gr.at[d], where))
        sends[-1].start()

    for cp in weight_copies:
        cp.wait()
    for k0 in range(0, wg.shape[0], 128):
        wgt[:, k0:k0 + 128] = wg[k0:k0 + 128, :].T
        wut[:, k0:k0 + 128] = wu[k0:k0 + 128, :].T
        wdt[k0:k0 + 128, :] = wd[:, k0:k0 + 128].T

    for d in range(1, ny):
        src = (y + ny - d) % ny
        remote(ibuf.at[src], ibuf.at[src], isem.at[d], ir.at[d], dev(src, x, z, c)).wait_recv()

    row_e = iota((n_in, ny * 8), 0)
    col_e = iota((n_in, ny * 8), 1)
    expand = ((row_e // 16 == col_e // 8) & (row_e % 4 == col_e % 8)).astype(F32).astype(BF16)
    known = dot(expand, ibuf[...].reshape(ny * 8, 128).astype(BF16))
    ri = iota((n_in, n_out), 0)
    lo = iota((n_in, n_out), 1)
    expert_o = (lo // 32) * 4 + (lo // 4) % 4
    target = (y * per_group + expert_o).astype(F32)
    slot_o = (lo % 2).astype(F32)
    same = ((ri // 4) % 2 == (lo // 2) % 2) & ((ri // 8) % 2 == (lo // 16) % 2)
    picked = jnp.zeros((n_in, n_out), F32)
    weight = jnp.zeros((n_in, n_out), F32)
    for k in range(top_k):
        hit = known[:, k:k + 1] == target
        picked = jnp.where(hit, 1.0, picked)
        weight = jnp.where(hit, known[:, top_k + k:top_k + k + 1], weight)
    rb = iota((n_in, n_in), 0)
    cb = iota((n_in, n_in), 1)
    earlier = (((cb // 16) * 4 + cb % 4) < ((rb // 16) * 4 + rb % 4)) & ((cb // 4) % 4 == 0)
    before = dot(earlier.astype(F32).astype(BF16), picked.astype(BF16))
    select = jnp.where((before == slot_o) & (picked > 0.0), 1.0, 0.0)
    pick_t = jnp.where(same, select, 0.0)
    pick_matrix = pick_t.T.astype(BF16)
    weight_matrix = (pick_t * weight).astype(BF16)

    for d in range(1, ny):
        src = (y + ny - d) % ny
        remote(gbuf.at[src], gbuf.at[src], gs.at[d], gr.at[d], dev(src, x, z, c)).wait_recv()
    packed[...] = dot(pick_matrix, gbuf[...].reshape(n_in, width)).astype(BF16).reshape(nx, 32, width)

    for d in range(1, nx):
        to = (x + d) % nx
        sends.append(remote(packed.at[to], xbuf.at[x], xs.at[d], xr.at[d], dev(y, to, z, c)))
        sends[-1].start()
    xbuf[x] = packed[x]
    for d in range(1, nx):
        src = (x + nx - d) % nx
        remote(packed.at[src], xbuf.at[src], xs.at[d], xr.at[d], dev(y, src, z, c)).wait_recv()
    rm = iota((n_out, n_out), 0)
    cm = iota((n_out, n_out), 1)

    def x_row(m):
        return ((m // 2) % nx) * 32 + ((m // half_m) % 2) * 16 + (m // rows_m) * 4 + ((m // quart_m) % 2) * 2 + m % 2

    to_quad = (cm == x_row(rm)).astype(F32).astype(BF16)
    from_quad = (rm == x_row(cm)).astype(F32).astype(BF16)
    mbuf[...] = dot(to_quad, xbuf[...].reshape(n_out, width)).astype(BF16).reshape(4, rows_m, width)

    zbuf[c, 6 + r] = mbuf[q]
    q1 = (q + 1) % 4
    q2 = (q + 2) % 4
    q3 = (q + 3) % 4
    end2 = jnp.where(r >= 2, 0, 3)
    id2 = (r + 14) % 16
    direct = [
        remote(mbuf.at[q2], zbuf.at[c, id2], zds.at[0], zr.at[id2], dev(y, x, 4 * q2 + end2, c)),
        remote(mbuf.at[q1], zbuf.at[c, r + 2], zds.at[1], zr.at[r + 2], dev(y, x, 4 * q1, c)),
        remote(mbuf.at[q3], zbuf.at[c, r + 10], zds.at[2], zr.at[r + 10], dev(y, x, 4 * q3 + 3, c)),
    ]
    z_right = (z + 1) % NZ
    z_left = (z + NZ - 1) % NZ

    def to_right(i):
        return remote(zbuf.at[c, i], zbuf.at[c, i], zfr.at[i], zr.at[i], dev(y, x, z_right, c))

    def to_left(i):
        return remote(zbuf.at[c, i], zbuf.at[c, i], zfl.at[i], zr.at[i], dev(y, x, z_left, c))

    def to_core(i):
        return remote(zbuf.at[c, i], zbuf.at[c, i], cs.at[i], cr.at[i], dev(y, x, z, other))

    def arrived(i):
        to_right(i).wait_recv()

    own = 6 + r
    for cp in direct:
        cp.start()
    sends += direct

    @pl.when(r < 3)
    def _():
        to_right(own).start()

    @pl.when(r > 0)
    def _():
        to_left(own).start()

    to_core(own).start()
    for k in range(1, 4):
        @pl.when(r >= k)
        def _():
            arrived(6 + r - k)

            @pl.when(r < 3)
            def _():
                to_right(6 + r - k).start()

            to_core(6 + r - k).start()

        @pl.when(r + k < 4)
        def _():
            arrived(6 + r + k)

            @pl.when(r > 0)
            def _():
                to_left(6 + r + k).start()

            to_core(6 + r + k).start()

    for j in range(6):
        right_id, left_id = 5 - j, 10 + j
        arrived(right_id)

        @pl.when(r < 3)
        def _():
            to_right(right_id).start()

        to_core(right_id).start()
        arrived(left_id)

        @pl.when(r > 0)
        def _():
            to_left(left_id).start()

        to_core(left_id).start()

    for i in range(16):
        remote(zbuf.at[other, i], zbuf.at[other, i], cs.at[i], cr.at[i], dev(y, x, z, other)).wait_recv()

    gate = up = back = None
    for cc in range(2):
        for h in range(2):
            rows = zbuf[cc, :, h * half_m:(h + 1) * half_m, :].reshape(16 * half_m, width)
            k0 = (2 * cc + h) * width
            parts = [dot(rows, w[k0:k0 + width, :]) for w in (wg, wu, wdt)]
            if gate is None:
                gate, up, back = parts
            else:
                gate, up, back = gate + parts[0], up + parts[1], back + parts[2]
    n_slot = 16 * quart_m
    units = wg.shape[1]
    gate = gate.reshape(16, 2, quart_m, units)[:, 0].reshape(n_slot, units)
    up = up.reshape(16, 2, quart_m, units)[:, 0].reshape(n_slot, units)
    back = back.reshape(16, 2, quart_m, units)[:, 1].reshape(n_slot, units)
    sig = jax.nn.sigmoid(gate)
    active = gate * sig
    hidden = (active * up).astype(BF16)
    gate_back = (back * up * sig * (1.0 + gate * (1.0 - sig))).astype(BF16)
    up_back = (back * active).astype(BF16)
    for cc in (other, c):
        for h in range(2):
            k0 = pl.multiple_of(cc * (2 * width) + h * width, 128)
            part_out = dot(hidden, wd[:, pl.ds(k0, width)])
            part_in = dot(gate_back, wgt[:, pl.ds(k0, width)]) + dot(up_back, wut[:, pl.ds(k0, width)])
            both = jnp.stack(
                [part_out.reshape(16, quart_m, width), part_in.reshape(16, quart_m, width)], axis=1
            ).reshape(16, half_m, width)
            obuf[cc, :, h * half_m:(h + 1) * half_m, :] = both.astype(BF16)
        if cc is other:
            for n, (lo_id, hi_id) in enumerate(((0, 6), (10, 16), (6, 10))):
                span = pl.ds(lo_id, hi_id - lo_id)
                sends.append(remote(obuf.at[other, span], pin.at[span], ps.at[n], pr.at[n], dev(y, x, z, other)))
                sends[-1].start()

    def pin_arrived(n):
        lo_id, hi_id = ((0, 6), (10, 16), (6, 10))[n]
        span = pl.ds(lo_id, hi_id - lo_id)
        remote(obuf.at[other, span], pin.at[span], ps.at[n], pr.at[n], dev(y, x, z, other)).wait_recv()

    def mine(i):
        return obuf[c, i].astype(F32) + pin[i].astype(F32)

    def out_left(i):
        return remote(cbuf.at[i], in_left.at[i], los.at[i], lor.at[i], dev(y, x, z_left, c))

    def out_right(i):
        return remote(cbuf.at[i], in_right.at[i - 6], ros.at[i - 6], ror.at[i - 6], dev(y, x, z_right, c))

    def out_final(i):
        dq = 1 if 2 <= i < 6 else 3 if 10 <= i < 14 else 2
        return remote(cbuf.at[i], fin.at[q], fs.at[i], fr.at[dq], dev(y, x, (4 * q + 10 + i) % NZ, c))

    pin_arrived(0)
    pin_arrived(1)
    for j in range(6):
        i = j

        @pl.when(r == 3)
        def _():
            cbuf[i] = mine(i).astype(BF16)
            out_left(i).start()

        @pl.when(r < 3)
        def _():
            out_left(i).wait_recv()
            cbuf[i] = (mine(i) + in_left[i].astype(F32)).astype(BF16)

            @pl.when(r > 0)
            def _():
                out_left(i).start()

            @pl.when(r == 0)
            def _():
                out_final(i).start()

        k = 15 - j

        @pl.when(r == 0)
        def _():
            cbuf[k] = mine(k).astype(BF16)
            out_right(k).start()

        @pl.when(r > 0)
        def _():
            out_right(k).wait_recv()
            cbuf[k] = (mine(k) + in_right[k - 6].astype(F32)).astype(BF16)

            @pl.when(r < 3)
            def _():
                out_right(k).start()

            @pl.when(r == 3)
            def _():
                out_final(k).start()

    pin_arrived(2)
    for n in range(4):
        i = 6 + n

        @pl.when(r == n)
        def _():
            total = mine(i)
            if n < 3:
                out_left(i).wait_recv()
                total = total + in_left[i].astype(F32)
            if n > 0:
                out_right(i).wait_recv()
                total = total + in_right[i - 6].astype(F32)
            fin[q] = total.astype(BF16)

        @pl.when(r > n)
        def _():
            @pl.when(r == 3)
            def _():
                cbuf[i] = mine(i).astype(BF16)

            @pl.when(r < 3)
            def _():
                out_left(i).wait_recv()
                cbuf[i] = (mine(i) + in_left[i].astype(F32)).astype(BF16)

            out_left(i).start()

        @pl.when(r < n)
        def _():
            @pl.when(r == 0)
            def _():
                cbuf[i] = mine(i).astype(BF16)

            @pl.when(r > 0)
            def _():
                out_right(i).wait_recv()
                cbuf[i] = (mine(i) + in_right[i - 6].astype(F32)).astype(BF16)

            out_right(i).start()

    for dq in range(1, 4):
        src = (q + dq) % 4
        remote(cbuf.at[0], fin.at[src], fs.at[0], fr.at[dq], dev(y, x, z_right, c)).wait_recv()

    rp[...] = dot(from_quad, fin[...].reshape(n_out, width)).astype(BF16).reshape(nx, 32, width)
    for d in range(1, nx):
        to = (x + d) % nx
        sends.append(remote(rp.at[to], ret.at[x], xbs.at[d], xbr.at[d], dev(y, to, z, c)))
        sends[-1].start()
    ret[x] = rp[x]
    for d in range(1, nx):
        src = (x + nx - d) % nx
        remote(rp.at[src], ret.at[src], xbs.at[d], xbr.at[d], dev(y, src, z, c)).wait_recv()

    returned = ret[...].reshape(n_out, width)
    ymsg[...] = dot(weight_matrix, returned).astype(BF16).reshape(ny, 16, width)
    for d in range(1, ny):
        to = (y + d) % ny
        sends.append(remote(ymsg.at[to], ybuf.at[y], ys.at[d], yr.at[d], dev(to, x, z, c)))
        sends[-1].start()
    ybuf[y] = ymsg[y]
    products = dot_nt(packed[...].reshape(n_out, width), returned)
    slot_score = jnp.sum(
        jnp.where((rm == cm + 2) & ((cm // 2) % 2 == 0), products, 0.0), axis=0, keepdims=True
    )
    token_score = jnp.where((select > 0.0) & ((lo // 2) % 2 == 0), slot_score, 0.0)
    lane = iota((n_in, 128), 1)
    scores = jnp.zeros((n_in, 128), F32)
    for k in range(top_k):
        of_pick = jnp.sum(jnp.where(known[:, k:k + 1] == target, token_score, 0.0), axis=1, keepdims=True)
        scores = jnp.where(lane == k, of_pick, scores)
    smsg[...] = scores.reshape(ny, 16, 128)[:, 0:8, :]
    for d in range(1, ny):
        to = (y + d) % ny
        for cc in range(2):
            sends.append(remote(
                smsg.at[to], sbuf.at[c, y], ss.at[2 * d + cc], sr.at[2 * d + c], dev(to, x, z, cc)
            ))
            sends[-1].start()
    sends.append(remote(smsg.at[y], sbuf.at[c, y], ss.at[0], sr.at[0], dev(y, x, z, other)))
    sends[-1].start()
    sbuf[c, y] = smsg[y]
    for d in range(1, ny):
        src = (y + ny - d) % ny
        remote(ymsg.at[src], ybuf.at[src], ys.at[d], yr.at[d], dev(src, x, z, c)).wait_recv()
    total = jnp.zeros((16, width), F32)
    for n in range(ny):
        total = total + ybuf[n].astype(F32)
    for h in range(2):
        mixed_ref[:, h * width:(h + 1) * width] = total[h * 8:h * 8 + 4].astype(BF16)
        grad_ref[:, h * width:(h + 1) * width] = total[h * 8 + 4:h * 8 + 8].astype(BF16)
    remote(smsg.at[y], sbuf.at[other, y], ss.at[0], sr.at[0], dev(y, x, z, other)).wait_recv()
    for d in range(1, ny):
        src = (y + ny - d) % ny
        for cc in range(2):
            remote(
                smsg.at[src], sbuf.at[cc, src], ss.at[2 * d + cc], sr.at[2 * d + cc], dev(src, x, z, cc)
            ).wait_recv()
    score = jnp.sum(sbuf[...].reshape(2 * ny, 8, 128), axis=0)[0:4]
    share = top_k // 2
    score_ref[...] = jnp.where(c == 0, score[:, 0:share], score[:, share:2 * share])

    for cp in sends:
        cp.wait_send()
    for i in range(16):
        to_core(i).wait_send()
        goes_right = r < 3 if i < 6 else (r < 3) & (r >= i - 6) if i < 10 else None
        goes_left = r > 0 if i >= 10 else (r > 0) & (r <= i - 6) if i >= 6 else None
        back_left = r > 0 if i < 6 else r > i - 6 if i < 10 else None
        back_right = r < 3 if i >= 10 else r < i - 6 if i >= 6 else None
        for cond, cp in ((goes_right, to_right), (goes_left, to_left), (back_left, out_left), (back_right, out_right)):
            if cond is not None:
                @pl.when(cond)
                def _():
                    cp(i).wait_send()
        if i < 6 or i >= 10:
            @pl.when(r == (0 if i < 6 else 3))
            def _():
                out_final(i).wait_send()


def body(tokens, cotangent, group_ids, expert_ids, gate_weights, w_gate, w_up, w_down):
    ny = lax.axis_size("group")
    nx = lax.axis_size("expert") // NZ
    depth = tokens.shape[1]
    units = w_gate.shape[2]
    width = depth // 4
    rows_m = 8 * nx
    dma = pltpu.SemaphoreType.DMA
    vmem = pl.BlockSpec(memory_space=pltpu.VMEM)
    hbm = pl.BlockSpec(memory_space=pl.ANY)

    def buf(*shape):
        return pltpu.VMEM(shape, BF16)

    scratch = [
        buf(depth, units), buf(depth, units), buf(units, depth),
        buf(depth, units), buf(units, depth), buf(units, depth),
        pltpu.VMEM((16, width), F32), buf(ny, 16, width), pltpu.VMEM((ny, 8, 128), F32),
        buf(nx, 32, width), buf(nx, 32, width), buf(4, rows_m, width),
        buf(2, 16, rows_m, width), buf(2, 16, rows_m, width), buf(16, rows_m, width), buf(16, rows_m, width),
        buf(10, rows_m, width), buf(10, rows_m, width),
        buf(4, rows_m, width), buf(nx, 32, width), buf(nx, 32, width),
        buf(ny, 16, width), buf(ny, 16, width),
        pltpu.VMEM((ny, 8, 128), F32), pltpu.VMEM((2, ny, 8, 128), F32),
        dma((3,)), dma((ny,)), dma((ny,)), dma((ny,)), dma((ny,)),
        dma((nx,)), dma((nx,)), dma((3,)), dma((16,)), dma((16,)), dma((16,)), dma((16,)), dma((16,)),
        dma((3,)), dma((3,)),
        dma((10,)), dma((10,)), dma((10,)), dma((10,)), dma((16,)), dma((4,)),
        dma((nx,)), dma((nx,)), dma((ny,)), dma((ny,)), dma((2 * ny,)), dma((2 * ny,)),
    ]
    return pl.pallas_call(
        functools.partial(kernel, ny, nx, 4 * nx),
        out_shape=(
            jax.ShapeDtypeStruct((tokens.shape[0], depth // 2), BF16),
            jax.ShapeDtypeStruct((tokens.shape[0], depth // 2), BF16),
            jax.ShapeDtypeStruct((tokens.shape[0], expert_ids.shape[1] // 2), F32),
        ),
        in_specs=[vmem] * 5 + [hbm] * 3,
        out_specs=(vmem, vmem, vmem),
        scratch_shapes=scratch,
        compiler_params=pltpu.CompilerParams(
            collective_id=0, has_side_effects=True, vmem_limit_bytes=40 * 1024 * 1024
        ),
    )(tokens, cotangent, group_ids, expert_ids, gate_weights, w_gate, w_up, w_down)


def solution(mesh):
    rows = P(("group", "expert"), None)
    return jax.shard_map(
        body,
        mesh=mesh,
        in_specs=(
            rows, rows, rows, rows, rows,
            P(("group", "expert"), None, "ffn"),
            P(("group", "expert"), None, "ffn"),
            P(("group", "expert"), "ffn", None),
        ),
        out_specs=(
            P(("group", "expert"), "ffn"),
            P(("group", "expert"), "ffn"),
            P(("group", "expert"), "ffn"),
        ),
        check_vma=False,
    )
```

```python
import functools

import jax
import jax.numpy as jnp
from jax import lax
from jax.experimental import pallas as pl
from jax.experimental.pallas import tpu as pltpu
from jax.sharding import PartitionSpec as P

NZ = 16
RELAY_HOP = 7
RELAY_GAP = 5
COLLECT_HOP = 4
COLLECT_GAP = 5
FINISH_HOP = 4
MESH = pl.DeviceIdType.MESH
F32 = jnp.float32
BF16 = jnp.bfloat16


def iota(shape, dim):
    return lax.broadcasted_iota(jnp.int32, shape, dim)


def dot(a, b):
    return jnp.dot(a, b, preferred_element_type=F32)


def dot_nt(a, b):
    return lax.dot_general(a, b, (((1,), (1,)), ((), ())), preferred_element_type=F32)


def kernel(
    ny, nx, per_group,
    tok_hbm, cot_hbm, gid_hbm, eid_hbm, gw_hbm, wg_hbm, wu_hbm, wd_hbm,
    mixed_hbm, grad_hbm, score_hbm,
    tok_ref, cot_ref, gid_ref, eid_ref, gw_ref, mixed_ref, grad_ref, score_ref,
    wg, wu, wd, wdt, wgt, wut,
    msg32, gbuf, ibuf, packed, xbuf, mbuf, zbuf, obuf, pin, cbuf, in_left, in_right,
    fin, rp, ret, ymsg, ybuf, smsg, sbuf, half_score, whole_score,
    asem, osem, wsem, gs, gr, isem, ir, xs, xr, zds, zr, zfr, zfl, cs, cr, ps, pr,
    los, lor, ros, ror, fs, fr, xbs, xbr, ys, yr, ss, sr, hs, hr,
):
    y = lax.axis_index("group")
    e = lax.axis_index("expert")
    c = lax.axis_index("ffn")
    x = e // NZ
    z = e % NZ
    q = z // 4
    r = z % 4
    other = 1 - c
    width = msg32.shape[1]
    top_k = eid_ref.shape[1]
    rows_m = mbuf.shape[1]
    half_m = rows_m // 2
    quart_m = rows_m // 4
    n_in = ny * 16
    n_out = nx * 32
    first = (width // 128 + 1) // 2 * 128
    chunks = (pl.ds(0, first), pl.ds(first, width - first))
    both_chunks = range(2)

    def dev(yy, xx, zz, cc):
        return (yy, xx * NZ + zz, cc)

    def remote(src, dst, send, recv, where):
        return pltpu.make_async_remote_copy(
            src_ref=src, dst_ref=dst, send_sem=send, recv_sem=recv,
            device_id=where, device_id_type=MESH,
        )

    inputs = [
        pltpu.make_async_copy(src, dst, asem.at[k])
        for k, (src, dst) in enumerate((
            (tok_hbm, tok_ref), (cot_hbm, cot_ref), (gid_hbm, gid_ref), (eid_hbm, eid_ref), (gw_hbm, gw_ref),
        ))
    ]
    for cp in inputs:
        cp.start()

    weight_copies = [
        pltpu.make_async_copy(wg_hbm.at[0], wg, wsem.at[0]),
        pltpu.make_async_copy(wu_hbm.at[0], wu, wsem.at[1]),
        pltpu.make_async_copy(wd_hbm.at[0], wd, wsem.at[2]),
    ]
    for cp in weight_copies:
        cp.start()

    barrier = pltpu.get_barrier_semaphore()
    q1 = (q + 1) % 4
    q2 = (q + 2) % 4
    q3 = (q + 3) % 4
    end2 = jnp.where(r >= 2, 0, 3)
    z_right = (z + 1) % NZ
    z_left = (z + NZ - 1) % NZ

    def greet(where):
        pl.semaphore_signal(barrier, inc=1, device_id=where, device_id_type=MESH)

    greet(dev(y, x, z, other))
    for d in range(1, ny):
        greet(dev((y + d) % ny, x, z, c))
    for d in range(1, nx):
        greet(dev(y, (x + d) % nx, z, c))

    def greet_z(d):
        greet(dev(y, x, (z + NZ + d) % NZ, c))

    @pl.when(r == 0)
    def _():
        for d in (1, 4, -1, -2, -3, -4, -5, -6):
            greet_z(d)

    @pl.when(r == 3)
    def _():
        for d in (-1, -4, 1, 2, 3, 4, 5, 6):
            greet_z(d)

    @pl.when((r == 1) | (r == 2))
    def _():
        greet_z(1)
        greet_z(-1)
        greet(dev(y, x, 4 * q1, c))
        greet(dev(y, x, 4 * q2 + end2, c))
        greet(dev(y, x, 4 * q3 + 3, c))

    for cp in inputs:
        cp.wait()

    for h in range(2):
        for a, ref in enumerate((tok_ref, cot_ref)):
            start = pl.multiple_of(c * (2 * width) + h * width, 128)
            msg32[h * 8 + a * 4:h * 8 + a * 4 + 4, :] = ref[:, pl.ds(start, width)].astype(F32)
    gbuf[y] = msg32[...].astype(BF16)
    lane4 = iota((4, 128), 1)
    gid = gid_ref[...].astype(F32)
    eid = eid_ref[...].astype(F32)
    gw = gw_ref[...].astype(F32)
    info = jnp.zeros((4, 128), F32)
    for k in range(top_k):
        ident = gid[:, k // 2:k // 2 + 1] * float(per_group) + eid[:, k:k + 1]
        info = jnp.where(lane4 == k, ident, info)
        info = jnp.where(lane4 == top_k + k, gw[:, k:k + 1], info)
    ibuf[y] = jnp.full((8, 128), -1.0, F32)
    ibuf[y, 0:4, :] = info

    pl.semaphore_wait(barrier, ny + nx - 1 + jnp.where((r == 0) | (r == 3), 8, 5))

    def gather_info(d, to, src):
        return remote(ibuf.at[src], ibuf.at[src], isem.at[d], ir.at[d], dev(to, x, z, c))

    def gather_rows(d, n, to, src):
        part = gbuf.at[src, :, chunks[n]]
        return remote(part, part, gs.at[n, d], gr.at[n, d], dev(to, x, z, c))

    sends = []

    def send(cp):
        cp.start()
        sends.append(cp)

    for d in range(1, ny):
        send(gather_info(d, (y + d) % ny, y))
    for n in both_chunks:
        for d in range(1, ny):
            send(gather_rows(d, n, (y + d) % ny, y))

    for cp in weight_copies:
        cp.wait()

    def turn(i, carry):
        at = pl.ds(pl.multiple_of(i * 128, 128), 128)
        wgt[:, at] = wg[at, :].T
        wut[:, at] = wu[at, :].T
        wdt[at, :] = wd[:, at].T
        return carry

    lax.fori_loop(0, wg.shape[0] // 128, turn, 0)

    for d in range(1, ny):
        src = (y + ny - d) % ny
        gather_info(d, src, src).wait_recv()

    n_tok = ny * 8
    known = ibuf[...].reshape(n_tok, 128)
    lo = iota((n_tok, n_out), 1)
    target = (y * per_group + (lo // 32) * 4 + (lo // 4) % 4).astype(F32)
    picked = jnp.zeros((n_tok, n_out), F32)
    weight = jnp.zeros((n_tok, n_out), F32)
    for k in range(top_k):
        hit = known[:, k:k + 1] == target
        picked = jnp.where(hit, 1.0, picked)
        weight = jnp.where(hit, known[:, top_k + k:top_k + k + 1], weight)
    earlier = (iota((n_tok, n_tok), 1) < iota((n_tok, n_tok), 0)).astype(F32).astype(BF16)
    before = dot(earlier, picked.astype(BF16))
    select = jnp.where((before == (lo % 2).astype(F32)) & (picked > 0.0), 1.0, 0.0)
    row_e = iota((n_in, n_tok), 0)
    col_e = iota((n_in, n_tok), 1)
    expand = ((row_e // 16 == col_e // 8) & (row_e % 4 == col_e % 8)).astype(F32).astype(BF16)
    ri = iota((n_in, n_out), 0)
    li = iota((n_in, n_out), 1)
    same = ((ri // 4) % 2 == (li // 2) % 2) & ((ri // 8) % 2 == (li // 16) % 2)
    pick_matrix = jnp.where(same, dot(expand, select.astype(BF16)), 0.0).T.astype(BF16)
    weight_matrix = jnp.where(same, dot(expand, (select * weight).astype(BF16)), 0.0).astype(BF16)

    rm = iota((n_out, n_out), 0)
    cm = iota((n_out, n_out), 1)

    def x_row(m):
        return ((m // 2) % nx) * 32 + ((m // half_m) % 2) * 16 + (m // rows_m) * 4 + ((m // quart_m) % 2) * 2 + m % 2

    to_quad = (cm == x_row(rm)).astype(F32).astype(BF16)
    from_quad = (rm == x_row(cm)).astype(F32).astype(BF16)

    def x_out(d, n, to, src):
        return remote(
            packed.at[to, :, chunks[n]], xbuf.at[src, :, chunks[n]], xs.at[n, d], xr.at[n, d], dev(y, to, z, c)
        )

    for n in both_chunks:
        for d in range(1, ny):
            src = (y + ny - d) % ny
            gather_rows(d, n, src, src).wait_recv()
        rows = gbuf[:, :, chunks[n]].reshape(n_in, chunks[n].size)
        packed[:, :, chunks[n]] = dot(pick_matrix, rows).astype(BF16).reshape(nx, 32, chunks[n].size)
        for d in range(1, nx):
            send(x_out(d, n, (x + d) % nx, x))
        xbuf[x, :, chunks[n]] = packed[x, :, chunks[n]]

    own = 6 + r
    id2 = (r + 14) % 16

    def along(i, n, sem, to):
        part = zbuf.at[c, i, :, chunks[n]]
        return remote(part, part, sem.at[n, i], zr.at[n, i], dev(y, x, to, c))

    def to_right(i, n):
        return along(i, n, zfr, z_right)

    def to_left(i, n):
        return along(i, n, zfl, z_left)

    def across(i, n, half):
        part = zbuf.at[half, i, :, chunks[n]]
        return remote(part, part, cs.at[n, i], cr.at[n, i], dev(y, x, z, other))

    def enter(n, k, quad, slot, where):
        return remote(
            mbuf.at[quad, :, chunks[n]], zbuf.at[c, slot, :, chunks[n]], zds.at[n, k], zr.at[n, slot],
            dev(y, x, where, c),
        )

    for n in both_chunks:
        for d in range(1, nx):
            src = (x + nx - d) % nx
            x_out(d, n, src, src).wait_recv()
        rows = xbuf[:, :, chunks[n]].reshape(n_out, chunks[n].size)
        mbuf[:, :, chunks[n]] = dot(to_quad, rows).astype(BF16).reshape(4, rows_m, chunks[n].size)
        zbuf[c, own, :, chunks[n]] = mbuf[q, :, chunks[n]]

        @pl.when(r < 3)
        def _():
            to_right(own, n).start()

        @pl.when(r > 0)
        def _():
            to_left(own, n).start()

        send(enter(n, 1, q1, r + 2, 4 * q1))
        send(enter(n, 2, q3, r + 10, 4 * q3 + 3))
        send(enter(n, 0, q2, id2, 4 * q2 + end2))
        across(own, n, c).start()

    def relay(t, carry):
        for n in both_chunks:
            u = t - n * RELAY_GAP
            for rank, step, ends, onward in ((r, -1, r < 3, to_right), (3 - r, 1, r > 0, to_left)):
                near = (u >= 1) & (u <= RELAY_HOP * rank) & (u % RELAY_HOP == 0)
                late = u - RELAY_HOP * (rank + 1)
                far = (late >= 0) & (late < 6)
                i = own + step * jnp.where(near, u // RELAY_HOP, rank + 1 + late)

                @pl.when(near | far)
                def _():
                    onward(i, n).wait_recv()

                    @pl.when(ends)
                    def _():
                        onward(i, n).start()

                    across(i, n, c).start()

        return carry

    lax.fori_loop(1, RELAY_GAP + 4 * RELAY_HOP + 6, relay, 0)

    def other_half(i, carry):
        for n in both_chunks:
            across(i, n, other).wait_recv()
        return carry

    lax.fori_loop(0, 16, other_half, 0)

    gate = up = back = None
    for cc in range(2):
        for h in range(2):
            rows = zbuf[cc, :, h * half_m:(h + 1) * half_m, :].reshape(16 * half_m, width)
            k0 = (2 * cc + h) * width
            parts = [dot(rows, w[k0:k0 + width, :]) for w in (wg, wu, wdt)]
            if gate is None:
                gate, up, back = parts
            else:
                gate, up, back = gate + parts[0], up + parts[1], back + parts[2]
    n_slot = 16 * quart_m
    units = wg.shape[1]
    gate = gate.reshape(16, 2, quart_m, units)[:, 0].reshape(n_slot, units)
    up = up.reshape(16, 2, quart_m, units)[:, 0].reshape(n_slot, units)
    back = back.reshape(16, 2, quart_m, units)[:, 1].reshape(n_slot, units)
    sig = jax.nn.sigmoid(gate)
    active = gate * sig
    hidden = (active * up).astype(BF16)
    gate_back = (back * up * sig * (1.0 + gate * (1.0 - sig))).astype(BF16)
    up_back = (back * active).astype(BF16)

    def partner_sum(n):
        return remote(
            obuf.at[other, :, :, chunks[n]], pin.at[:, :, chunks[n]], ps.at[n], pr.at[n], dev(y, x, z, other)
        )

    for n in both_chunks:
        size = chunks[n].size
        for half in (other, c):
            for h in range(2):
                at = pl.ds(pl.multiple_of(half * (2 * width) + h * width + chunks[n].start, 128), size)
                part_out = dot(hidden, wd[:, at])
                part_in = dot(gate_back, wgt[:, at]) + dot(up_back, wut[:, at])
                both = jnp.stack(
                    [part_out.reshape(16, quart_m, size), part_in.reshape(16, quart_m, size)], axis=1
                ).reshape(16, half_m, size)
                obuf[half, :, h * half_m:(h + 1) * half_m, chunks[n]] = both.astype(BF16)
            if half is other:
                send(partner_sum(n))

    def mine(i, n):
        return obuf[c, i, :, chunks[n]].astype(F32) + pin[i, :, chunks[n]].astype(F32)

    def out_left(i, n):
        return remote(
            cbuf.at[i, :, chunks[n]], in_left.at[i, :, chunks[n]], los.at[n, i], lor.at[n, i], dev(y, x, z_left, c)
        )

    def out_right(i, n):
        return remote(
            cbuf.at[i, :, chunks[n]], in_right.at[i - 6, :, chunks[n]], ros.at[n, i - 6], ror.at[n, i - 6],
            dev(y, x, z_right, c),
        )

    def out_final(i, n, dq):
        return remote(
            cbuf.at[i, :, chunks[n]], fin.at[q, :, chunks[n]], fs.at[n, i], fr.at[n, dq],
            dev(y, x, (4 * q + 10 + i) % NZ, c),
        )

    def collect(t, carry):
        for n in both_chunks:
            u = t - n * COLLECT_GAP
            for rank, step, outward, landed in ((3 - r, 1, out_left, in_left), (r, -1, out_right, in_right)):
                k = u - COLLECT_HOP * rank
                i = k if step == 1 else 15 - k
                slot = i if step == 1 else i - 6

                @pl.when((k >= 0) & (k < 9 - rank))
                def _():
                    @pl.when(rank == 0)
                    def _():
                        cbuf[i, :, chunks[n]] = mine(i, n).astype(BF16)

                    @pl.when(rank > 0)
                    def _():
                        outward(i, n).wait_recv()
                        cbuf[i, :, chunks[n]] = (mine(i, n) + landed[slot, :, chunks[n]].astype(F32)).astype(BF16)

                    @pl.when(rank < 3)
                    def _():
                        outward(i, n).start()

                    @pl.when(rank == 3)
                    def _():
                        out_final(i, n, jnp.where(k < 2, 2, 2 - step)).start()

        return carry

    def finish_own(n):
        @pl.when(r == 0)
        def _():
            out_left(own, n).wait_recv()
            fin[q, :, chunks[n]] = (mine(own, n) + in_left[own, :, chunks[n]].astype(F32)).astype(BF16)

        @pl.when(r == 3)
        def _():
            out_right(own, n).wait_recv()
            fin[q, :, chunks[n]] = (mine(own, n) + in_right[r, :, chunks[n]].astype(F32)).astype(BF16)

        @pl.when((r > 0) & (r < 3))
        def _():
            out_left(own, n).wait_recv()
            out_right(own, n).wait_recv()
            fin[q, :, chunks[n]] = (
                mine(own, n) + in_left[own, :, chunks[n]].astype(F32) + in_right[r, :, chunks[n]].astype(F32)
            ).astype(BF16)

    def x_back(d, n, to, src):
        return remote(
            rp.at[to, :, chunks[n]], ret.at[src, :, chunks[n]], xbs.at[n, d], xbr.at[n, d], dev(y, to, z, c)
        )

    def finish_z(n):
        finish_own(n)
        for dq in range(1, 4):
            part = fin.at[(q + dq) % 4, :, chunks[n]]
            remote(part, part, fs.at[n, 0], fr.at[n, dq], dev(y, x, z_right, c)).wait_recv()
        rows = fin[:, :, chunks[n]].reshape(n_out, chunks[n].size)
        rp[:, :, chunks[n]] = dot(from_quad, rows).astype(BF16).reshape(nx, 32, chunks[n].size)
        for d in range(1, nx):
            send(x_back(d, n, (x + d) % nx, x))
        ret[x, :, chunks[n]] = rp[x, :, chunks[n]]

    def y_back(d, n, to, src):
        return remote(
            ymsg.at[to, :, chunks[n]], ybuf.at[src, :, chunks[n]], ys.at[n, d], yr.at[n, d], dev(to, x, z, c)
        )

    def finish_x(n):
        for d in range(1, nx):
            src = (x + nx - d) % nx
            x_back(d, n, src, src).wait_recv()
        rows = ret[:, :, chunks[n]].reshape(n_out, chunks[n].size)
        ymsg[:, :, chunks[n]] = dot(weight_matrix, rows).astype(BF16).reshape(ny, 16, chunks[n].size)
        for d in range(1, ny):
            send(y_back(d, n, (y + d) % ny, y))
        ybuf[y, :, chunks[n]] = ymsg[y, :, chunks[n]]
        return dot_nt(packed[:, :, chunks[n]].reshape(n_out, chunks[n].size), rows)

    partner_sum(0).wait_recv()
    partner_sum(1).wait_recv()
    first_done = 9 + 3 * COLLECT_HOP + FINISH_HOP
    last = COLLECT_GAP + 9 + 3 * COLLECT_HOP
    lax.fori_loop(0, first_done, collect, 0)
    finish_z(0)
    lax.fori_loop(first_done, first_done + FINISH_HOP, collect, 0)
    products = finish_x(0)
    if last > first_done + FINISH_HOP:
        lax.fori_loop(first_done + FINISH_HOP, last, collect, 0)
    finish_z(1)
    products = products + finish_x(1)

    slot_score = jnp.sum(
        jnp.where((rm == cm + 2) & ((cm // 2) % 2 == 0), products, 0.0), axis=0, keepdims=True
    )
    token_score = jnp.where((select > 0.0) & ((lo // 2) % 2 == 0), slot_score, 0.0)
    lane = iota((n_tok, 128), 1)
    scores = jnp.zeros((n_tok, 128), F32)
    for k in range(top_k):
        of_pick = jnp.sum(jnp.where(known[:, k:k + 1] == target, token_score, 0.0), axis=1, keepdims=True)
        scores = jnp.where(lane == k, of_pick, scores)
    smsg[...] = scores.reshape(ny, 8, 128)

    def score_back(d, to, src):
        return remote(smsg.at[to], sbuf.at[src], ss.at[d], sr.at[d], dev(to, x, z, c))

    for d in range(1, ny):
        send(score_back(d, (y + d) % ny, y))
    sbuf[y] = smsg[y]
    for d in range(1, ny):
        src = (y + ny - d) % ny
        score_back(d, src, src).wait_recv()
    half_score[...] = jnp.sum(sbuf[...], axis=0)
    to_partner = remote(half_score, whole_score, hs.at[0], hr.at[0], dev(y, x, z, other))
    send(to_partner)
    for n in both_chunks:
        for d in range(1, ny):
            src = (y + ny - d) % ny
            y_back(d, n, src, src).wait_recv()
    total = jnp.zeros((16, width), F32)
    for n in range(ny):
        total = total + ybuf[n].astype(F32)
    for h in range(2):
        mixed_ref[:, h * width:(h + 1) * width] = total[h * 8:h * 8 + 4].astype(BF16)
        grad_ref[:, h * width:(h + 1) * width] = total[h * 8 + 4:h * 8 + 8].astype(BF16)
    to_partner.wait_recv()
    score = (half_score[...] + whole_score[...])[0:4]
    outputs = [
        pltpu.make_async_copy(src, dst, osem.at[k])
        for k, (src, dst) in enumerate(((mixed_ref, mixed_hbm), (grad_ref, grad_hbm), (score_ref, score_hbm)))
    ]
    outputs[0].start()
    outputs[1].start()
    share = top_k // 2
    score_ref[...] = jnp.where(c == 0, score[:, 0:share], score[:, share:2 * share])
    outputs[2].start()

    for cp in sends:
        cp.wait_send()

    def sent(i, carry):
        near_right = (i >= 6) & (r >= i - 6) | (i < 6)
        near_left = (i < 10) & (r <= i - 6) | (i >= 10)
        for n in both_chunks:
            across(i, n, c).wait_send()

            @pl.when((r < 3) & near_right)
            def _():
                to_right(i, n).wait_send()

            @pl.when((r > 0) & near_left)
            def _():
                to_left(i, n).wait_send()

            @pl.when((r > 0) & (i < 6) | (i >= 6) & (r > i - 6))
            def _():
                out_left(i, n).wait_send()

            @pl.when((r < 3) & (i >= 10) | (i < 10) & (r < i - 6))
            def _():
                out_right(i, n).wait_send()

            @pl.when((r == 0) & (i < 6) | (r == 3) & (i >= 10))
            def _():
                out_final(i, n, 1).wait_send()

        return carry

    lax.fori_loop(0, 16, sent, 0)
    for cp in outputs:
        cp.wait()


def body(tokens, cotangent, group_ids, expert_ids, gate_weights, w_gate, w_up, w_down):
    ny = lax.axis_size("group")
    nx = lax.axis_size("expert") // NZ
    depth = tokens.shape[1]
    units = w_gate.shape[2]
    width = depth // 4
    rows_m = 8 * nx
    dma = pltpu.SemaphoreType.DMA
    hbm = pl.BlockSpec(memory_space=pl.ANY)

    def buf(*shape):
        return pltpu.VMEM(shape, BF16)

    n_tok, n_pick = expert_ids.shape
    small = [
        pltpu.VMEM(tokens.shape, BF16), pltpu.VMEM(cotangent.shape, BF16),
        pltpu.VMEM(group_ids.shape, jnp.int32), pltpu.VMEM(expert_ids.shape, jnp.int32),
        pltpu.VMEM(gate_weights.shape, BF16),
        pltpu.VMEM((n_tok, depth // 2), BF16), pltpu.VMEM((n_tok, depth // 2), BF16),
        pltpu.VMEM((n_tok, n_pick // 2), F32),
    ]
    scratch = small + [
        buf(depth, units), buf(depth, units), buf(units, depth),
        buf(depth, units), buf(units, depth), buf(units, depth),
        pltpu.VMEM((16, width), F32), buf(ny, 16, width), pltpu.VMEM((ny, 8, 128), F32),
        buf(nx, 32, width), buf(nx, 32, width), buf(4, rows_m, width),
        buf(2, 16, rows_m, width), buf(2, 16, rows_m, width), buf(16, rows_m, width), buf(16, rows_m, width),
        buf(10, rows_m, width), buf(10, rows_m, width),
        buf(4, rows_m, width), buf(nx, 32, width), buf(nx, 32, width),
        buf(ny, 16, width), buf(ny, 16, width),
        pltpu.VMEM((ny, 8, 128), F32), pltpu.VMEM((ny, 8, 128), F32),
        pltpu.VMEM((8, 128), F32), pltpu.VMEM((8, 128), F32),
        dma((5,)), dma((3,)), dma((3,)), dma((2, ny)), dma((2, ny)), dma((ny,)), dma((ny,)),
        dma((2, nx)), dma((2, nx)), dma((2, 3)), dma((2, 16)), dma((2, 16)), dma((2, 16)), dma((2, 16)), dma((2, 16)),
        dma((2,)), dma((2,)),
        dma((2, 10)), dma((2, 10)), dma((2, 10)), dma((2, 10)), dma((2, 16)), dma((2, 4)),
        dma((2, nx)), dma((2, nx)), dma((2, ny)), dma((2, ny)), dma((ny,)), dma((ny,)), dma((1,)), dma((1,)),
    ]
    return pl.pallas_call(
        functools.partial(kernel, ny, nx, 4 * nx),
        out_shape=(
            jax.ShapeDtypeStruct((tokens.shape[0], depth // 2), BF16),
            jax.ShapeDtypeStruct((tokens.shape[0], depth // 2), BF16),
            jax.ShapeDtypeStruct((tokens.shape[0], expert_ids.shape[1] // 2), F32),
        ),
        in_specs=[hbm] * 8,
        out_specs=(hbm, hbm, hbm),
        scratch_shapes=scratch,
        compiler_params=pltpu.CompilerParams(
            collective_id=0, has_side_effects=True, vmem_limit_bytes=60 * 1024 * 1024
        ),
    )(tokens, cotangent, group_ids, expert_ids, gate_weights, w_gate, w_up, w_down)


def solution(mesh):
    rows = P(("group", "expert"), None)
    return jax.shard_map(
        body,
        mesh=mesh,
        in_specs=(
            rows, rows, rows, rows, rows,
            P(("group", "expert"), None, "ffn"),
            P(("group", "expert"), None, "ffn"),
            P(("group", "expert"), "ffn", None),
        ),
        out_specs=(
            P(("group", "expert"), "ffn"),
            P(("group", "expert"), "ffn"),
            P(("group", "expert"), "ffn"),
        ),
        check_vma=False,
    )
```

```python
import functools

import jax
import jax.numpy as jnp
from jax import lax
from jax.experimental import pallas as pl
from jax.experimental.pallas import tpu as pltpu
from jax.sharding import PartitionSpec as P

NZ = 16
FIRST_TILES = 4
RELAY_HOP = 7
RELAY_GAP = 5
COLLECT_HOP = 5
COLLECT_GAP = 7
FINISH_HOP = 3
MESH = pl.DeviceIdType.MESH
F32 = jnp.float32
BF16 = jnp.bfloat16


def iota(shape, dim):
    return lax.broadcasted_iota(jnp.int32, shape, dim)


def dot(a, b):
    return jnp.dot(a, b, preferred_element_type=F32)


def dot_nt(a, b):
    return lax.dot_general(a, b, (((1,), (1,)), ((), ())), preferred_element_type=F32)


def kernel(
    ny, nx, per_group,
    tok_hbm, cot_hbm, gid_hbm, eid_hbm, gw_hbm, wg_hbm, wu_hbm, wd_hbm,
    mixed_hbm, grad_hbm, score_hbm,
    tok_ref, cot_ref, gid_ref, eid_ref, gw_ref, mixed_ref, grad_ref, score_ref,
    wg, wu, wd, wdt, wgt, wut,
    msg32, gbuf, ibuf, packed, xbuf, mbuf, zbuf, obuf, pin, cbuf, in_left, in_right,
    fin, rp, ret, ymsg, ybuf, smsg, sbuf, half_score, whole_score,
    asem, osem, wsem, gs, gr, isem, ir, xs, xr, zds, zr, zfr, zfl, cs, cr, ps, pr,
    los, lor, ros, ror, fs, fr, xbs, xbr, ys, yr, ss, sr, hs, hr,
):
    y = lax.axis_index("group")
    e = lax.axis_index("expert")
    c = lax.axis_index("ffn")
    x = e // NZ
    z = e % NZ
    q = z // 4
    r = z % 4
    other = 1 - c
    width = msg32.shape[1]
    top_k = eid_ref.shape[1]
    rows_m = mbuf.shape[1]
    half_m = rows_m // 2
    quart_m = rows_m // 4
    n_in = ny * 16
    n_out = nx * 32
    first = min(FIRST_TILES, width // 128 - 1) * 128
    chunks = (pl.ds(0, first), pl.ds(first, width - first))
    both_chunks = range(2)
    outward_order = (1, 0)

    def dev(yy, xx, zz, cc):
        return (yy, xx * NZ + zz, cc)

    def remote(src, dst, send, recv, where):
        return pltpu.make_async_remote_copy(
            src_ref=src, dst_ref=dst, send_sem=send, recv_sem=recv,
            device_id=where, device_id_type=MESH,
        )

    inputs = [
        pltpu.make_async_copy(src, dst, asem.at[k])
        for k, (src, dst) in enumerate((
            (tok_hbm, tok_ref), (cot_hbm, cot_ref), (gid_hbm, gid_ref), (eid_hbm, eid_ref), (gw_hbm, gw_ref),
        ))
    ]
    for cp in inputs:
        cp.start()

    weight_copies = [
        pltpu.make_async_copy(wg_hbm.at[0], wg, wsem.at[0]),
        pltpu.make_async_copy(wu_hbm.at[0], wu, wsem.at[1]),
        pltpu.make_async_copy(wd_hbm.at[0], wd, wsem.at[2]),
    ]
    for cp in weight_copies:
        cp.start()

    barrier = pltpu.get_barrier_semaphore()
    q1 = (q + 1) % 4
    q2 = (q + 2) % 4
    q3 = (q + 3) % 4
    end2 = jnp.where(r >= 2, 0, 3)
    z_right = (z + 1) % NZ
    z_left = (z + NZ - 1) % NZ

    def greet(where):
        pl.semaphore_signal(barrier, inc=1, device_id=where, device_id_type=MESH)

    greet(dev(y, x, z, other))
    for d in range(1, ny):
        greet(dev((y + d) % ny, x, z, c))
    for d in range(1, nx):
        greet(dev(y, (x + d) % nx, z, c))

    def greet_z(d):
        greet(dev(y, x, (z + NZ + d) % NZ, c))

    @pl.when(r == 0)
    def _():
        for d in (1, 4, -1, -2, -3, -4, -5, -6):
            greet_z(d)

    @pl.when(r == 3)
    def _():
        for d in (-1, -4, 1, 2, 3, 4, 5, 6):
            greet_z(d)

    @pl.when((r == 1) | (r == 2))
    def _():
        greet_z(1)
        greet_z(-1)
        greet(dev(y, x, 4 * q1, c))
        greet(dev(y, x, 4 * q2 + end2, c))
        greet(dev(y, x, 4 * q3 + 3, c))

    for cp in inputs:
        cp.wait()

    for h in range(2):
        for a, ref in enumerate((tok_ref, cot_ref)):
            start = pl.multiple_of(c * (2 * width) + h * width, 128)
            msg32[h * 8 + a * 4:h * 8 + a * 4 + 4, :] = ref[:, pl.ds(start, width)].astype(F32)
    gbuf[y] = msg32[...].astype(BF16)
    lane4 = iota((4, 128), 1)
    gid = gid_ref[...].astype(F32)
    eid = eid_ref[...].astype(F32)
    gw = gw_ref[...].astype(F32)
    info = jnp.zeros((4, 128), F32)
    for k in range(top_k):
        ident = gid[:, k // 2:k // 2 + 1] * float(per_group) + eid[:, k:k + 1]
        info = jnp.where(lane4 == k, ident, info)
        info = jnp.where(lane4 == top_k + k, gw[:, k:k + 1], info)
    ibuf[y] = jnp.full((8, 128), -1.0, F32)
    ibuf[y, 0:4, :] = info

    pl.semaphore_wait(barrier, ny + nx - 1 + jnp.where((r == 0) | (r == 3), 8, 5))

    def gather_info(d, to, src):
        return remote(ibuf.at[src], ibuf.at[src], isem.at[d], ir.at[d], dev(to, x, z, c))

    def gather_rows(d, n, to, src):
        part = gbuf.at[src, :, chunks[n]]
        return remote(part, part, gs.at[n, d], gr.at[n, d], dev(to, x, z, c))

    sends = []

    def send(cp):
        cp.start()
        sends.append(cp)

    for d in range(1, ny):
        send(gather_info(d, (y + d) % ny, y))
    for n in outward_order:
        for d in range(1, ny):
            send(gather_rows(d, n, (y + d) % ny, y))

    for cp in weight_copies:
        cp.wait()

    def turn(i, carry):
        at = pl.ds(pl.multiple_of(i * 128, 128), 128)
        wgt[:, at] = wg[at, :].T
        wut[:, at] = wu[at, :].T
        wdt[at, :] = wd[:, at].T
        return carry

    lax.fori_loop(0, wg.shape[0] // 128, turn, 0)

    for d in range(1, ny):
        src = (y + ny - d) % ny
        gather_info(d, src, src).wait_recv()

    n_tok = ny * 8
    known = ibuf[...].reshape(n_tok, 128)
    lo = iota((n_tok, n_out), 1)
    target = (y * per_group + (lo // 32) * 4 + (lo // 4) % 4).astype(F32)
    picked = jnp.zeros((n_tok, n_out), F32)
    weight = jnp.zeros((n_tok, n_out), F32)
    for k in range(top_k):
        hit = known[:, k:k + 1] == target
        picked = jnp.where(hit, 1.0, picked)
        weight = jnp.where(hit, known[:, top_k + k:top_k + k + 1], weight)
    earlier = (iota((n_tok, n_tok), 1) < iota((n_tok, n_tok), 0)).astype(F32).astype(BF16)
    before = dot(earlier, picked.astype(BF16))
    select = jnp.where((before == (lo % 2).astype(F32)) & (picked > 0.0), 1.0, 0.0)
    row_e = iota((n_in, n_tok), 0)
    col_e = iota((n_in, n_tok), 1)
    expand = ((row_e // 16 == col_e // 8) & (row_e % 4 == col_e % 8)).astype(F32).astype(BF16)
    ri = iota((n_in, n_out), 0)
    li = iota((n_in, n_out), 1)
    same = ((ri // 4) % 2 == (li // 2) % 2) & ((ri // 8) % 2 == (li // 16) % 2)
    pick_matrix = jnp.where(same, dot(expand, select.astype(BF16)), 0.0).T.astype(BF16)
    weight_matrix = jnp.where(same, dot(expand, (select * weight).astype(BF16)), 0.0).astype(BF16)

    rm = iota((n_out, n_out), 0)
    cm = iota((n_out, n_out), 1)

    def x_row(m):
        return ((m // 2) % nx) * 32 + ((m // half_m) % 2) * 16 + (m // rows_m) * 4 + ((m // quart_m) % 2) * 2 + m % 2

    to_quad = (cm == x_row(rm)).astype(F32).astype(BF16)
    from_quad = (rm == x_row(cm)).astype(F32).astype(BF16)

    def x_out(d, n, to, src):
        return remote(
            packed.at[to, :, chunks[n]], xbuf.at[src, :, chunks[n]], xs.at[n, d], xr.at[n, d], dev(y, to, z, c)
        )

    for n in outward_order:
        for d in range(1, ny):
            src = (y + ny - d) % ny
            gather_rows(d, n, src, src).wait_recv()
        rows = gbuf[:, :, chunks[n]].reshape(n_in, chunks[n].size)
        packed[:, :, chunks[n]] = dot(pick_matrix, rows).astype(BF16).reshape(nx, 32, chunks[n].size)
        for d in range(1, nx):
            send(x_out(d, n, (x + d) % nx, x))
        xbuf[x, :, chunks[n]] = packed[x, :, chunks[n]]

    own = 6 + r
    id2 = (r + 14) % 16

    def along(i, n, sem, to):
        part = zbuf.at[c, i, :, chunks[n]]
        return remote(part, part, sem.at[n, i], zr.at[n, i], dev(y, x, to, c))

    def to_right(i, n):
        return along(i, n, zfr, z_right)

    def to_left(i, n):
        return along(i, n, zfl, z_left)

    def across(i, n, half):
        part = zbuf.at[half, i, :, chunks[n]]
        return remote(part, part, cs.at[n, i], cr.at[n, i], dev(y, x, z, other))

    def enter(n, k, quad, slot, where):
        return remote(
            mbuf.at[quad, :, chunks[n]], zbuf.at[c, slot, :, chunks[n]], zds.at[n, k], zr.at[n, slot],
            dev(y, x, where, c),
        )

    for n in outward_order:
        for d in range(1, nx):
            src = (x + nx - d) % nx
            x_out(d, n, src, src).wait_recv()
        rows = xbuf[:, :, chunks[n]].reshape(n_out, chunks[n].size)
        mbuf[:, :, chunks[n]] = dot(to_quad, rows).astype(BF16).reshape(4, rows_m, chunks[n].size)
        zbuf[c, own, :, chunks[n]] = mbuf[q, :, chunks[n]]

        @pl.when(r < 3)
        def _():
            to_right(own, n).start()

        @pl.when(r > 0)
        def _():
            to_left(own, n).start()

        send(enter(n, 1, q1, r + 2, 4 * q1))
        send(enter(n, 2, q3, r + 10, 4 * q3 + 3))
        send(enter(n, 0, q2, id2, 4 * q2 + end2))
        across(own, n, c).start()

    def relay(t, carry):
        for n in outward_order:
            u = t - (1 - n) * RELAY_GAP
            for rank, step, ends, onward in ((r, -1, r < 3, to_right), (3 - r, 1, r > 0, to_left)):
                near = (u >= 1) & (u <= RELAY_HOP * rank) & (u % RELAY_HOP == 0)
                late = u - RELAY_HOP * (rank + 1)
                far = (late >= 0) & (late < 6)
                i = own + step * jnp.where(near, u // RELAY_HOP, rank + 1 + late)

                @pl.when(near | far)
                def _():
                    onward(i, n).wait_recv()

                    @pl.when(ends)
                    def _():
                        onward(i, n).start()

                    across(i, n, c).start()

        return carry

    lax.fori_loop(1, RELAY_GAP + 4 * RELAY_HOP + 6, relay, 0)

    def other_half(i, carry):
        for n in both_chunks:
            across(i, n, other).wait_recv()
        return carry

    gate = up = back = None
    for half in (c, other):
        if half is other:
            lax.fori_loop(0, 16, other_half, 0)
        for h in range(2):
            rows = zbuf[half, :, h * half_m:(h + 1) * half_m, :].reshape(16 * half_m, width)
            at = pl.ds(pl.multiple_of(half * (2 * width) + h * width, 128), width)
            parts = [dot(rows, w[at, :]) for w in (wg, wu, wdt)]
            if gate is None:
                gate, up, back = parts
            else:
                gate, up, back = gate + parts[0], up + parts[1], back + parts[2]
    n_slot = 16 * quart_m
    units = wg.shape[1]
    gate = gate.reshape(16, 2, quart_m, units)[:, 0].reshape(n_slot, units)
    up = up.reshape(16, 2, quart_m, units)[:, 0].reshape(n_slot, units)
    back = back.reshape(16, 2, quart_m, units)[:, 1].reshape(n_slot, units)
    sig = jax.nn.sigmoid(gate)
    active = gate * sig
    hidden = (active * up).astype(BF16)
    gate_back = (back * up * sig * (1.0 + gate * (1.0 - sig))).astype(BF16)
    up_back = (back * active).astype(BF16)

    def partner_sum(n):
        return remote(
            obuf.at[other, :, :, chunks[n]], pin.at[:, :, chunks[n]], ps.at[n], pr.at[n], dev(y, x, z, other)
        )

    def produce(half, n):
        size = chunks[n].size
        for h in range(2):
            at = pl.ds(pl.multiple_of(half * (2 * width) + h * width + chunks[n].start, 128), size)
            part_out = dot(hidden, wd[:, at])
            part_in = dot(gate_back, wgt[:, at]) + dot(up_back, wut[:, at])
            both = jnp.stack(
                [part_out.reshape(16, quart_m, size), part_in.reshape(16, quart_m, size)], axis=1
            ).reshape(16, half_m, size)
            obuf[half, :, h * half_m:(h + 1) * half_m, chunks[n]] = both.astype(BF16)

    produce(other, 0)
    send(partner_sum(0))
    produce(c, 0)
    produce(other, 1)
    send(partner_sum(1))

    def mine(i, n):
        return obuf[c, i, :, chunks[n]].astype(F32) + pin[i, :, chunks[n]].astype(F32)

    def out_left(i, n):
        return remote(
            cbuf.at[i, :, chunks[n]], in_left.at[i, :, chunks[n]], los.at[n, i], lor.at[n, i], dev(y, x, z_left, c)
        )

    def out_right(i, n):
        return remote(
            cbuf.at[i, :, chunks[n]], in_right.at[i - 6, :, chunks[n]], ros.at[n, i - 6], ror.at[n, i - 6],
            dev(y, x, z_right, c),
        )

    def out_final(i, n, dq):
        return remote(
            cbuf.at[i, :, chunks[n]], fin.at[q, :, chunks[n]], fs.at[n, i], fr.at[n, dq],
            dev(y, x, (4 * q + 10 + i) % NZ, c),
        )

    def collect(t, carry):
        for n in both_chunks:
            u = t - n * COLLECT_GAP
            for rank, step, outward, landed in ((3 - r, 1, out_left, in_left), (r, -1, out_right, in_right)):
                k = u - COLLECT_HOP * rank
                i = k if step == 1 else 15 - k
                slot = i if step == 1 else i - 6

                @pl.when((k >= 0) & (k < 9 - rank))
                def _():
                    @pl.when(rank == 0)
                    def _():
                        cbuf[i, :, chunks[n]] = mine(i, n).astype(BF16)

                    @pl.when(rank > 0)
                    def _():
                        outward(i, n).wait_recv()
                        cbuf[i, :, chunks[n]] = (mine(i, n) + landed[slot, :, chunks[n]].astype(F32)).astype(BF16)

                    @pl.when(rank < 3)
                    def _():
                        outward(i, n).start()

                    @pl.when(rank == 3)
                    def _():
                        out_final(i, n, jnp.where(k < 2, 2, 2 - step)).start()

        return carry

    def finish_own(n):
        @pl.when(r == 0)
        def _():
            out_left(own, n).wait_recv()
            fin[q, :, chunks[n]] = (mine(own, n) + in_left[own, :, chunks[n]].astype(F32)).astype(BF16)

        @pl.when(r == 3)
        def _():
            out_right(own, n).wait_recv()
            fin[q, :, chunks[n]] = (mine(own, n) + in_right[r, :, chunks[n]].astype(F32)).astype(BF16)

        @pl.when((r > 0) & (r < 3))
        def _():
            out_left(own, n).wait_recv()
            out_right(own, n).wait_recv()
            fin[q, :, chunks[n]] = (
                mine(own, n) + in_left[own, :, chunks[n]].astype(F32) + in_right[r, :, chunks[n]].astype(F32)
            ).astype(BF16)

    def x_back(d, n, to, src):
        return remote(
            rp.at[to, :, chunks[n]], ret.at[src, :, chunks[n]], xbs.at[n, d], xbr.at[n, d], dev(y, to, z, c)
        )

    def finish_z(n):
        finish_own(n)
        for dq in range(1, 4):
            part = fin.at[(q + dq) % 4, :, chunks[n]]
            remote(part, part, fs.at[n, 0], fr.at[n, dq], dev(y, x, z_right, c)).wait_recv()
        rows = fin[:, :, chunks[n]].reshape(n_out, chunks[n].size)
        rp[:, :, chunks[n]] = dot(from_quad, rows).astype(BF16).reshape(nx, 32, chunks[n].size)
        for d in range(1, nx):
            send(x_back(d, n, (x + d) % nx, x))
        ret[x, :, chunks[n]] = rp[x, :, chunks[n]]

    def y_back(d, n, to, src):
        return remote(
            ymsg.at[to, :, chunks[n]], ybuf.at[src, :, chunks[n]], ys.at[n, d], yr.at[n, d], dev(to, x, z, c)
        )

    def finish_x(n):
        for d in range(1, nx):
            src = (x + nx - d) % nx
            x_back(d, n, src, src).wait_recv()
        rows = ret[:, :, chunks[n]].reshape(n_out, chunks[n].size)
        ymsg[:, :, chunks[n]] = dot(weight_matrix, rows).astype(BF16).reshape(ny, 16, chunks[n].size)
        for d in range(1, ny):
            send(y_back(d, n, (y + d) % ny, y))
        ybuf[y, :, chunks[n]] = ymsg[y, :, chunks[n]]
        return dot_nt(packed[:, :, chunks[n]].reshape(n_out, chunks[n].size), rows)

    partner_sum(0).wait_recv()
    first_done = 9 + 3 * COLLECT_HOP + FINISH_HOP
    last = COLLECT_GAP + 9 + 3 * COLLECT_HOP
    lax.fori_loop(0, COLLECT_GAP, collect, 0)
    produce(c, 1)
    partner_sum(1).wait_recv()
    lax.fori_loop(COLLECT_GAP, first_done, collect, 0)
    finish_z(0)
    lax.fori_loop(first_done, first_done + FINISH_HOP, collect, 0)
    products = finish_x(0)
    if last > first_done + FINISH_HOP:
        lax.fori_loop(first_done + FINISH_HOP, last, collect, 0)
    finish_z(1)
    products = products + finish_x(1)

    slot_score = jnp.sum(
        jnp.where((rm == cm + 2) & ((cm // 2) % 2 == 0), products, 0.0), axis=0, keepdims=True
    )
    token_score = jnp.where((select > 0.0) & ((lo // 2) % 2 == 0), slot_score, 0.0)
    lane = iota((n_tok, 128), 1)
    scores = jnp.zeros((n_tok, 128), F32)
    for k in range(top_k):
        of_pick = jnp.sum(jnp.where(known[:, k:k + 1] == target, token_score, 0.0), axis=1, keepdims=True)
        scores = jnp.where(lane == k, of_pick, scores)
    smsg[...] = scores.reshape(ny, 8, 128)

    def score_back(d, to, src):
        return remote(smsg.at[to], sbuf.at[src], ss.at[d], sr.at[d], dev(to, x, z, c))

    for d in range(1, ny):
        send(score_back(d, (y + d) % ny, y))
    sbuf[y] = smsg[y]
    for d in range(1, ny):
        src = (y + ny - d) % ny
        score_back(d, src, src).wait_recv()
    half_score[...] = jnp.sum(sbuf[...], axis=0)
    to_partner = remote(half_score, whole_score, hs.at[0], hr.at[0], dev(y, x, z, other))
    send(to_partner)
    for n in both_chunks:
        for d in range(1, ny):
            src = (y + ny - d) % ny
            y_back(d, n, src, src).wait_recv()
    total = jnp.zeros((16, width), F32)
    for n in range(ny):
        total = total + ybuf[n].astype(F32)
    for h in range(2):
        mixed_ref[:, h * width:(h + 1) * width] = total[h * 8:h * 8 + 4].astype(BF16)
        grad_ref[:, h * width:(h + 1) * width] = total[h * 8 + 4:h * 8 + 8].astype(BF16)
    to_partner.wait_recv()
    score = (half_score[...] + whole_score[...])[0:4]
    outputs = [
        pltpu.make_async_copy(src, dst, osem.at[k])
        for k, (src, dst) in enumerate(((mixed_ref, mixed_hbm), (grad_ref, grad_hbm), (score_ref, score_hbm)))
    ]
    outputs[0].start()
    outputs[1].start()
    share = top_k // 2
    score_ref[...] = jnp.where(c == 0, score[:, 0:share], score[:, share:2 * share])
    outputs[2].start()

    for cp in sends:
        cp.wait_send()

    def sent(i, carry):
        near_right = (i >= 6) & (r >= i - 6) | (i < 6)
        near_left = (i < 10) & (r <= i - 6) | (i >= 10)
        for n in both_chunks:
            across(i, n, c).wait_send()

            @pl.when((r < 3) & near_right)
            def _():
                to_right(i, n).wait_send()

            @pl.when((r > 0) & near_left)
            def _():
                to_left(i, n).wait_send()

            @pl.when((r > 0) & (i < 6) | (i >= 6) & (r > i - 6))
            def _():
                out_left(i, n).wait_send()

            @pl.when((r < 3) & (i >= 10) | (i < 10) & (r < i - 6))
            def _():
                out_right(i, n).wait_send()

            @pl.when((r == 0) & (i < 6) | (r == 3) & (i >= 10))
            def _():
                out_final(i, n, 1).wait_send()

        return carry

    lax.fori_loop(0, 16, sent, 0)
    for cp in outputs:
        cp.wait()


def body(tokens, cotangent, group_ids, expert_ids, gate_weights, w_gate, w_up, w_down):
    ny = lax.axis_size("group")
    nx = lax.axis_size("expert") // NZ
    depth = tokens.shape[1]
    units = w_gate.shape[2]
    width = depth // 4
    rows_m = 8 * nx
    dma = pltpu.SemaphoreType.DMA
    hbm = pl.BlockSpec(memory_space=pl.ANY)

    def buf(*shape):
        return pltpu.VMEM(shape, BF16)

    n_tok, n_pick = expert_ids.shape
    small = [
        pltpu.VMEM(tokens.shape, BF16), pltpu.VMEM(cotangent.shape, BF16),
        pltpu.VMEM(group_ids.shape, jnp.int32), pltpu.VMEM(expert_ids.shape, jnp.int32),
        pltpu.VMEM(gate_weights.shape, BF16),
        pltpu.VMEM((n_tok, depth // 2), BF16), pltpu.VMEM((n_tok, depth // 2), BF16),
        pltpu.VMEM((n_tok, n_pick // 2), F32),
    ]
    scratch = small + [
        buf(depth, units), buf(depth, units), buf(units, depth),
        buf(depth, units), buf(units, depth), buf(units, depth),
        pltpu.VMEM((16, width), F32), buf(ny, 16, width), pltpu.VMEM((ny, 8, 128), F32),
        buf(nx, 32, width), buf(nx, 32, width), buf(4, rows_m, width),
        buf(2, 16, rows_m, width), buf(2, 16, rows_m, width), buf(16, rows_m, width), buf(16, rows_m, width),
        buf(10, rows_m, width), buf(10, rows_m, width),
        buf(4, rows_m, width), buf(nx, 32, width), buf(nx, 32, width),
        buf(ny, 16, width), buf(ny, 16, width),
        pltpu.VMEM((ny, 8, 128), F32), pltpu.VMEM((ny, 8, 128), F32),
        pltpu.VMEM((8, 128), F32), pltpu.VMEM((8, 128), F32),
        dma((5,)), dma((3,)), dma((3,)), dma((2, ny)), dma((2, ny)), dma((ny,)), dma((ny,)),
        dma((2, nx)), dma((2, nx)), dma((2, 3)), dma((2, 16)), dma((2, 16)), dma((2, 16)), dma((2, 16)), dma((2, 16)),
        dma((2,)), dma((2,)),
        dma((2, 10)), dma((2, 10)), dma((2, 10)), dma((2, 10)), dma((2, 16)), dma((2, 4)),
        dma((2, nx)), dma((2, nx)), dma((2, ny)), dma((2, ny)), dma((ny,)), dma((ny,)), dma((1,)), dma((1,)),
    ]
    return pl.pallas_call(
        functools.partial(kernel, ny, nx, 4 * nx),
        out_shape=(
            jax.ShapeDtypeStruct((tokens.shape[0], depth // 2), BF16),
            jax.ShapeDtypeStruct((tokens.shape[0], depth // 2), BF16),
            jax.ShapeDtypeStruct((tokens.shape[0], expert_ids.shape[1] // 2), F32),
        ),
        in_specs=[hbm] * 8,
        out_specs=(hbm, hbm, hbm),
        scratch_shapes=scratch,
        compiler_params=pltpu.CompilerParams(
            collective_id=0, has_side_effects=True, vmem_limit_bytes=60 * 1024 * 1024
        ),
    )(tokens, cotangent, group_ids, expert_ids, gate_weights, w_gate, w_up, w_down)


def solution(mesh):
    rows = P(("group", "expert"), None)
    return jax.shard_map(
        body,
        mesh=mesh,
        in_specs=(
            rows, rows, rows, rows, rows,
            P(("group", "expert"), None, "ffn"),
            P(("group", "expert"), None, "ffn"),
            P(("group", "expert"), "ffn", None),
        ),
        out_specs=(
            P(("group", "expert"), "ffn"),
            P(("group", "expert"), "ffn"),
            P(("group", "expert"), "ffn"),
        ),
        check_vma=False,
    )
```

```python
import functools

import jax
import jax.numpy as jnp
from jax import lax
from jax.experimental import pallas as pl
from jax.experimental.pallas import tpu as pltpu
from jax.sharding import PartitionSpec as P

NZ = 16
FIRST_TILES = 4
RELAY_HOP = 8
RELAY_GAP = 7
COLLECT_HOP = 4
COLLECT_GAP = 7
FINISH_HOP = 2
MESH = pl.DeviceIdType.MESH
F32 = jnp.float32
BF16 = jnp.bfloat16


def iota(shape, dim):
    return lax.broadcasted_iota(jnp.int32, shape, dim)


def dot(a, b):
    return jnp.dot(a, b, preferred_element_type=F32)


def dot_nt(a, b):
    return lax.dot_general(a, b, (((1,), (1,)), ((), ())), preferred_element_type=F32)


def kernel(
    ny, nx, per_group,
    tok_hbm, cot_hbm, gid_hbm, eid_hbm, gw_hbm, wg_hbm, wu_hbm, wd_hbm,
    rows_hbm, score_hbm,
    tok_ref, cot_ref, gid_ref, eid_ref, gw_ref, rows_ref, score_ref,
    wg, wu, wd, wdt, wgt, wut,
    msg32, gbuf, ibuf, packed, xbuf, mbuf, zbuf, obuf, pin, cbuf, in_left, in_right,
    fin, rp, ret, ymsg, ybuf, smsg, sbuf, half_score, whole_score,
    asem, osem, wsem, gs, gr, isem, ir, xs, xr, zds, zr, zfr, zfl, cs, cr, ps, pr,
    los, lor, ros, ror, fs, fr, xbs, xbr, ys, yr, ss, sr, hs, hr,
):
    y = lax.axis_index("group")
    e = lax.axis_index("expert")
    c = lax.axis_index("ffn")
    x = e // NZ
    z = e % NZ
    q = z // 4
    r = z % 4
    other = 1 - c
    width = msg32.shape[1]
    top_k = eid_ref.shape[1]
    rows_m = mbuf.shape[1]
    half_m = rows_m // 2
    quart_m = rows_m // 4
    n_in = ny * 16
    n_out = nx * 32
    first = min(FIRST_TILES, width // 128 - 1) * 128
    chunks = (pl.ds(0, first), pl.ds(first, width - first))
    both_chunks = range(2)
    outward_order = (1, 0)

    def dev(yy, xx, zz, cc):
        return (yy, xx * NZ + zz, cc)

    def remote(src, dst, send, recv, where):
        return pltpu.make_async_remote_copy(
            src_ref=src, dst_ref=dst, send_sem=send, recv_sem=recv,
            device_id=where, device_id_type=MESH,
        )

    inputs = [
        pltpu.make_async_copy(src, dst, asem.at[k])
        for k, (src, dst) in enumerate((
            (tok_hbm, tok_ref), (cot_hbm, cot_ref), (gid_hbm, gid_ref), (eid_hbm, eid_ref), (gw_hbm, gw_ref),
        ))
    ]
    for cp in inputs:
        cp.start()

    weight_copies = [
        pltpu.make_async_copy(wg_hbm.at[0], wg, wsem.at[0]),
        pltpu.make_async_copy(wu_hbm.at[0], wu, wsem.at[1]),
        pltpu.make_async_copy(wd_hbm.at[0], wd, wsem.at[2]),
    ]
    for cp in weight_copies:
        cp.start()

    barrier = pltpu.get_barrier_semaphore()
    q1 = (q + 1) % 4
    q2 = (q + 2) % 4
    q3 = (q + 3) % 4
    end2 = jnp.where(r >= 2, 0, 3)
    z_right = (z + 1) % NZ
    z_left = (z + NZ - 1) % NZ

    def greet(where):
        pl.semaphore_signal(barrier, inc=1, device_id=where, device_id_type=MESH)

    greet(dev(y, x, z, other))
    for d in range(1, ny):
        greet(dev((y + d) % ny, x, z, c))
    for d in range(1, nx):
        greet(dev(y, (x + d) % nx, z, c))

    def greet_z(d):
        greet(dev(y, x, (z + NZ + d) % NZ, c))

    @pl.when(r == 0)
    def _():
        for d in (1, 4, -1, -2, -3, -4, -5, -6):
            greet_z(d)

    @pl.when(r == 3)
    def _():
        for d in (-1, -4, 1, 2, 3, 4, 5, 6):
            greet_z(d)

    @pl.when((r == 1) | (r == 2))
    def _():
        greet_z(1)
        greet_z(-1)
        greet(dev(y, x, 4 * q1, c))
        greet(dev(y, x, 4 * q2 + end2, c))
        greet(dev(y, x, 4 * q3 + 3, c))

    for cp in inputs:
        cp.wait()

    for h in range(2):
        for a, ref in enumerate((tok_ref, cot_ref)):
            start = pl.multiple_of(c * (2 * width) + h * width, 128)
            msg32[h * 8 + a * 4:h * 8 + a * 4 + 4, :] = ref[:, pl.ds(start, width)].astype(F32)
    gbuf[y] = msg32[...].astype(BF16)
    lane4 = iota((4, 128), 1)
    gid = gid_ref[...].astype(F32)
    eid = eid_ref[...].astype(F32)
    gw = gw_ref[...].astype(F32)
    info = jnp.zeros((4, 128), F32)
    for k in range(top_k):
        ident = gid[:, k // 2:k // 2 + 1] * float(per_group) + eid[:, k:k + 1]
        info = jnp.where(lane4 == k, ident, info)
        info = jnp.where(lane4 == top_k + k, gw[:, k:k + 1], info)
    ibuf[y] = jnp.full((8, 128), -1.0, F32)
    ibuf[y, 0:4, :] = info

    pl.semaphore_wait(barrier, ny + nx - 1 + jnp.where((r == 0) | (r == 3), 8, 5))

    def gather_info(d, to, src):
        return remote(ibuf.at[src], ibuf.at[src], isem.at[d], ir.at[d], dev(to, x, z, c))

    def gather_rows(d, n, to, src):
        part = gbuf.at[src, :, chunks[n]]
        return remote(part, part, gs.at[n, d], gr.at[n, d], dev(to, x, z, c))

    sends = []

    def send(cp):
        cp.start()
        sends.append(cp)

    for d in range(1, ny):
        send(gather_info(d, (y + d) % ny, y))
    for n in outward_order:
        for d in range(1, ny):
            send(gather_rows(d, n, (y + d) % ny, y))

    for cp in weight_copies:
        cp.wait()

    def turn(i, carry):
        at = pl.ds(pl.multiple_of(i * 128, 128), 128)
        wgt[:, at] = wg[at, :].T
        wut[:, at] = wu[at, :].T
        wdt[at, :] = wd[:, at].T
        return carry

    lax.fori_loop(0, wg.shape[0] // 128, turn, 0)

    for d in range(1, ny):
        src = (y + ny - d) % ny
        gather_info(d, src, src).wait_recv()

    n_tok = ny * 8
    known = ibuf[...].reshape(n_tok, 128)
    lo = iota((n_tok, n_out), 1)
    target = (y * per_group + (lo // 32) * 4 + (lo // 4) % 4).astype(F32)
    picked = jnp.zeros((n_tok, n_out), F32)
    weight = jnp.zeros((n_tok, n_out), F32)
    for k in range(top_k):
        hit = known[:, k:k + 1] == target
        picked = jnp.where(hit, 1.0, picked)
        weight = jnp.where(hit, known[:, top_k + k:top_k + k + 1], weight)
    earlier = (iota((n_tok, n_tok), 1) < iota((n_tok, n_tok), 0)).astype(F32).astype(BF16)
    before = dot(earlier, picked.astype(BF16))
    select = jnp.where((before == (lo % 2).astype(F32)) & (picked > 0.0), 1.0, 0.0)
    row_e = iota((n_in, n_tok), 0)
    col_e = iota((n_in, n_tok), 1)
    expand = ((row_e // 16 == col_e // 8) & (row_e % 4 == col_e % 8)).astype(F32).astype(BF16)
    ri = iota((n_in, n_out), 0)
    li = iota((n_in, n_out), 1)
    same = ((ri // 4) % 2 == (li // 2) % 2) & ((ri // 8) % 2 == (li // 16) % 2)
    pick_matrix = jnp.where(same, dot(expand, select.astype(BF16)), 0.0).T.astype(BF16)
    weight_matrix = jnp.where(same, dot(expand, (select * weight).astype(BF16)), 0.0).astype(BF16)

    rm = iota((n_out, n_out), 0)
    cm = iota((n_out, n_out), 1)

    def x_row(m):
        return ((m // 2) % nx) * 32 + ((m // half_m) % 2) * 16 + (m // rows_m) * 4 + ((m // quart_m) % 2) * 2 + m % 2

    to_quad = (cm == x_row(rm)).astype(F32).astype(BF16)
    from_quad = (rm == x_row(cm)).astype(F32).astype(BF16)

    def x_out(d, n, to, src):
        return remote(
            packed.at[to, :, chunks[n]], xbuf.at[src, :, chunks[n]], xs.at[n, d], xr.at[n, d], dev(y, to, z, c)
        )

    for n in outward_order:
        for d in range(1, ny):
            src = (y + ny - d) % ny
            gather_rows(d, n, src, src).wait_recv()
        rows = gbuf[:, :, chunks[n]].reshape(n_in, chunks[n].size)
        packed[:, :, chunks[n]] = dot(pick_matrix, rows).astype(BF16).reshape(nx, 32, chunks[n].size)
        for d in range(1, nx):
            send(x_out(d, n, (x + d) % nx, x))
        xbuf[x, :, chunks[n]] = packed[x, :, chunks[n]]

    own = 6 + r
    id2 = (r + 14) % 16

    def along(i, n, sem, to):
        part = zbuf.at[c, i, :, chunks[n]]
        return remote(part, part, sem.at[n, i], zr.at[n, i], dev(y, x, to, c))

    def to_right(i, n):
        return along(i, n, zfr, z_right)

    def to_left(i, n):
        return along(i, n, zfl, z_left)

    def across(i, n, half):
        part = zbuf.at[half, i, :, chunks[n]]
        return remote(part, part, cs.at[n, i], cr.at[n, i], dev(y, x, z, other))

    def enter(n, k, quad, slot, where):
        return remote(
            mbuf.at[quad, :, chunks[n]], zbuf.at[c, slot, :, chunks[n]], zds.at[n, k], zr.at[n, slot],
            dev(y, x, where, c),
        )

    for n in outward_order:
        for d in range(1, nx):
            src = (x + nx - d) % nx
            x_out(d, n, src, src).wait_recv()
        rows = xbuf[:, :, chunks[n]].reshape(n_out, chunks[n].size)
        mbuf[:, :, chunks[n]] = dot(to_quad, rows).astype(BF16).reshape(4, rows_m, chunks[n].size)
        zbuf[c, own, :, chunks[n]] = mbuf[q, :, chunks[n]]

        @pl.when(r < 3)
        def _():
            to_right(own, n).start()

        @pl.when(r > 0)
        def _():
            to_left(own, n).start()

        send(enter(n, 1, q1, r + 2, 4 * q1))
        send(enter(n, 2, q3, r + 10, 4 * q3 + 3))
        send(enter(n, 0, q2, id2, 4 * q2 + end2))
        across(own, n, c).start()

    def relay(t, carry):
        for n in outward_order:
            u = t - (1 - n) * RELAY_GAP
            for rank, step, ends, onward in ((r, -1, r < 3, to_right), (3 - r, 1, r > 0, to_left)):
                near = (u >= 1) & (u <= RELAY_HOP * rank) & (u % RELAY_HOP == 0)
                late = u - RELAY_HOP * (rank + 1)
                far = (late >= 0) & (late < 6)
                i = own + step * jnp.where(near, u // RELAY_HOP, rank + 1 + late)

                @pl.when(near | far)
                def _():
                    onward(i, n).wait_recv()

                    @pl.when(ends)
                    def _():
                        onward(i, n).start()

                    across(i, n, c).start()

        return carry

    lax.fori_loop(1, RELAY_GAP + 4 * RELAY_HOP + 6, relay, 0)

    def other_half(i, carry):
        for n in both_chunks:
            across(i, n, other).wait_recv()
        return carry

    gate = up = back = None
    for half in (c, other):
        if half is other:
            lax.fori_loop(0, 16, other_half, 0)
        for h in range(2):
            rows = zbuf[half, :, h * half_m:(h + 1) * half_m, :].reshape(16 * half_m, width)
            at = pl.ds(pl.multiple_of(half * (2 * width) + h * width, 128), width)
            parts = [dot(rows, w[at, :]) for w in (wg, wu, wdt)]
            if gate is None:
                gate, up, back = parts
            else:
                gate, up, back = gate + parts[0], up + parts[1], back + parts[2]
    n_slot = 16 * quart_m
    units = wg.shape[1]
    gate = gate.reshape(16, 2, quart_m, units)[:, 0].reshape(n_slot, units)
    up = up.reshape(16, 2, quart_m, units)[:, 0].reshape(n_slot, units)
    back = back.reshape(16, 2, quart_m, units)[:, 1].reshape(n_slot, units)
    sig = jax.nn.sigmoid(gate)
    active = gate * sig
    hidden = (active * up).astype(BF16)
    gate_back = (back * up * sig * (1.0 + gate * (1.0 - sig))).astype(BF16)
    up_back = (back * active).astype(BF16)

    def partner_sum(n):
        return remote(
            obuf.at[other, :, :, chunks[n]], pin.at[:, :, chunks[n]], ps.at[n], pr.at[n], dev(y, x, z, other)
        )

    def produce(half, n):
        size = chunks[n].size
        for h in range(2):
            at = pl.ds(pl.multiple_of(half * (2 * width) + h * width + chunks[n].start, 128), size)
            part_out = dot(hidden, wd[:, at])
            part_in = dot(gate_back, wgt[:, at]) + dot(up_back, wut[:, at])
            both = jnp.stack(
                [part_out.reshape(16, quart_m, size), part_in.reshape(16, quart_m, size)], axis=1
            ).reshape(16, half_m, size)
            obuf[half, :, h * half_m:(h + 1) * half_m, chunks[n]] = both.astype(BF16)

    produce(other, 0)
    send(partner_sum(0))
    produce(c, 0)

    def mine(i, n):
        return obuf[c, i, :, chunks[n]].astype(F32) + pin[i, :, chunks[n]].astype(F32)

    def out_left(i, n):
        return remote(
            cbuf.at[i, :, chunks[n]], in_left.at[i, :, chunks[n]], los.at[n, i], lor.at[n, i], dev(y, x, z_left, c)
        )

    def out_right(i, n):
        return remote(
            cbuf.at[i, :, chunks[n]], in_right.at[i - 6, :, chunks[n]], ros.at[n, i - 6], ror.at[n, i - 6],
            dev(y, x, z_right, c),
        )

    def out_final(i, n, dq):
        return remote(
            cbuf.at[i, :, chunks[n]], fin.at[q, :, chunks[n]], fs.at[n, i], fr.at[n, dq],
            dev(y, x, (4 * q + 10 + i) % NZ, c),
        )

    def collect(t, carry):
        for n in both_chunks:
            u = t - n * COLLECT_GAP
            for rank, step, outward, landed in ((3 - r, 1, out_left, in_left), (r, -1, out_right, in_right)):
                k = u - COLLECT_HOP * rank
                i = k if step == 1 else 15 - k
                slot = i if step == 1 else i - 6

                @pl.when((k >= 0) & (k < 9 - rank))
                def _():
                    @pl.when(rank == 0)
                    def _():
                        cbuf[i, :, chunks[n]] = mine(i, n).astype(BF16)

                    @pl.when(rank > 0)
                    def _():
                        outward(i, n).wait_recv()
                        cbuf[i, :, chunks[n]] = (mine(i, n) + landed[slot, :, chunks[n]].astype(F32)).astype(BF16)

                    @pl.when(rank < 3)
                    def _():
                        outward(i, n).start()

                    @pl.when(rank == 3)
                    def _():
                        out_final(i, n, jnp.where(k < 2, 2, 2 - step)).start()

        return carry

    def finish_own(n):
        @pl.when(r == 0)
        def _():
            out_left(own, n).wait_recv()
            fin[q, :, chunks[n]] = (mine(own, n) + in_left[own, :, chunks[n]].astype(F32)).astype(BF16)

        @pl.when(r == 3)
        def _():
            out_right(own, n).wait_recv()
            fin[q, :, chunks[n]] = (mine(own, n) + in_right[r, :, chunks[n]].astype(F32)).astype(BF16)

        @pl.when((r > 0) & (r < 3))
        def _():
            out_left(own, n).wait_recv()
            out_right(own, n).wait_recv()
            fin[q, :, chunks[n]] = (
                mine(own, n) + in_left[own, :, chunks[n]].astype(F32) + in_right[r, :, chunks[n]].astype(F32)
            ).astype(BF16)

    def x_back(d, n, to, src):
        return remote(
            rp.at[to, :, chunks[n]], ret.at[src, :, chunks[n]], xbs.at[n, d], xbr.at[n, d], dev(y, to, z, c)
        )

    def finish_z(n):
        finish_own(n)
        for dq in range(1, 4):
            part = fin.at[(q + dq) % 4, :, chunks[n]]
            remote(part, part, fs.at[n, 0], fr.at[n, dq], dev(y, x, z_right, c)).wait_recv()
        rows = fin[:, :, chunks[n]].reshape(n_out, chunks[n].size)
        rp[:, :, chunks[n]] = dot(from_quad, rows).astype(BF16).reshape(nx, 32, chunks[n].size)
        for d in range(1, nx):
            send(x_back(d, n, (x + d) % nx, x))
        ret[x, :, chunks[n]] = rp[x, :, chunks[n]]

    def y_back(d, n, to, src):
        return remote(
            ymsg.at[to, :, chunks[n]], ybuf.at[src, :, chunks[n]], ys.at[n, d], yr.at[n, d], dev(to, x, z, c)
        )

    def finish_x(n):
        for d in range(1, nx):
            src = (x + nx - d) % nx
            x_back(d, n, src, src).wait_recv()
        rows = ret[:, :, chunks[n]].reshape(n_out, chunks[n].size)
        ymsg[:, :, chunks[n]] = dot(weight_matrix, rows).astype(BF16).reshape(ny, 16, chunks[n].size)
        for d in range(1, ny):
            send(y_back(d, n, (y + d) % ny, y))
        ybuf[y, :, chunks[n]] = ymsg[y, :, chunks[n]]
        return dot_nt(packed[:, :, chunks[n]].reshape(n_out, chunks[n].size), rows)

    partner_sum(0).wait_recv()
    first_done = 9 + 3 * COLLECT_HOP + FINISH_HOP
    last = COLLECT_GAP + 9 + 3 * COLLECT_HOP
    lax.fori_loop(0, COLLECT_HOP, collect, 0)
    produce(other, 1)
    send(partner_sum(1))
    produce(c, 1)
    partner_sum(1).wait_recv()
    lax.fori_loop(COLLECT_HOP, first_done, collect, 0)
    finish_z(0)
    lax.fori_loop(first_done, first_done + FINISH_HOP, collect, 0)
    products = finish_x(0)
    if last > first_done + FINISH_HOP:
        lax.fori_loop(first_done + FINISH_HOP, last, collect, 0)
    finish_z(1)
    products = products + finish_x(1)

    slot_score = jnp.sum(
        jnp.where((rm == cm + 2) & ((cm // 2) % 2 == 0), products, 0.0), axis=0, keepdims=True
    )
    token_score = jnp.where((select > 0.0) & ((lo // 2) % 2 == 0), slot_score, 0.0)
    lane = iota((n_tok, 128), 1)
    scores = jnp.zeros((n_tok, 128), F32)
    for k in range(top_k):
        of_pick = jnp.sum(jnp.where(known[:, k:k + 1] == target, token_score, 0.0), axis=1, keepdims=True)
        scores = jnp.where(lane == k, of_pick, scores)
    smsg[...] = scores.reshape(ny, 8, 128)

    def score_back(d, to, src):
        return remote(smsg.at[to], sbuf.at[src], ss.at[d], sr.at[d], dev(to, x, z, c))

    for d in range(1, ny):
        send(score_back(d, (y + d) % ny, y))
    sbuf[y] = smsg[y]
    for d in range(1, ny):
        src = (y + ny - d) % ny
        score_back(d, src, src).wait_recv()
    half_score[...] = jnp.sum(sbuf[...], axis=0)
    to_partner = remote(half_score, whole_score, hs.at[0], hr.at[0], dev(y, x, z, other))
    send(to_partner)
    for n in both_chunks:
        for d in range(1, ny):
            src = (y + ny - d) % ny
            y_back(d, n, src, src).wait_recv()
    total = jnp.zeros((16, width), F32)
    for n in range(ny):
        total = total + ybuf[n].astype(F32)
    for h in range(2):
        rows_ref[:, h * width:(h + 1) * width] = total[h * 8:h * 8 + 4].astype(BF16)
        rows_ref[:, (2 + h) * width:(3 + h) * width] = total[h * 8 + 4:h * 8 + 8].astype(BF16)
    to_partner.wait_recv()
    score = (half_score[...] + whole_score[...])[0:4]
    outputs = [
        pltpu.make_async_copy(src, dst, osem.at[k])
        for k, (src, dst) in enumerate(((rows_ref, rows_hbm), (score_ref, score_hbm)))
    ]
    outputs[0].start()
    share = top_k // 2
    score_ref[...] = jnp.where(c == 0, score[:, 0:share], score[:, share:2 * share])
    outputs[1].start()

    for cp in sends:
        cp.wait_send()

    def sent(i, carry):
        near_right = (i >= 6) & (r >= i - 6) | (i < 6)
        near_left = (i < 10) & (r <= i - 6) | (i >= 10)
        for n in both_chunks:
            across(i, n, c).wait_send()

            @pl.when((r < 3) & near_right)
            def _():
                to_right(i, n).wait_send()

            @pl.when((r > 0) & near_left)
            def _():
                to_left(i, n).wait_send()

            @pl.when((r > 0) & (i < 6) | (i >= 6) & (r > i - 6))
            def _():
                out_left(i, n).wait_send()

            @pl.when((r < 3) & (i >= 10) | (i < 10) & (r < i - 6))
            def _():
                out_right(i, n).wait_send()

            @pl.when((r == 0) & (i < 6) | (r == 3) & (i >= 10))
            def _():
                out_final(i, n, 1).wait_send()

        return carry

    lax.fori_loop(0, 16, sent, 0)
    for cp in outputs:
        cp.wait()


def body(tokens, cotangent, group_ids, expert_ids, gate_weights, w_gate, w_up, w_down):
    ny = lax.axis_size("group")
    nx = lax.axis_size("expert") // NZ
    depth = tokens.shape[1]
    units = w_gate.shape[2]
    width = depth // 4
    rows_m = 8 * nx
    dma = pltpu.SemaphoreType.DMA
    hbm = pl.BlockSpec(memory_space=pl.ANY)

    def buf(*shape):
        return pltpu.VMEM(shape, BF16)

    n_tok, n_pick = expert_ids.shape
    small = [
        pltpu.VMEM(tokens.shape, BF16), pltpu.VMEM(cotangent.shape, BF16),
        pltpu.VMEM(group_ids.shape, jnp.int32), pltpu.VMEM(expert_ids.shape, jnp.int32),
        pltpu.VMEM(gate_weights.shape, BF16),
        pltpu.VMEM((n_tok, depth), BF16),
        pltpu.VMEM((n_tok, n_pick // 2), F32),
    ]
    scratch = small + [
        buf(depth, units), buf(depth, units), buf(units, depth),
        buf(depth, units), buf(units, depth), buf(units, depth),
        pltpu.VMEM((16, width), F32), buf(ny, 16, width), pltpu.VMEM((ny, 8, 128), F32),
        buf(nx, 32, width), buf(nx, 32, width), buf(4, rows_m, width),
        buf(2, 16, rows_m, width), buf(2, 16, rows_m, width), buf(16, rows_m, width), buf(16, rows_m, width),
        buf(10, rows_m, width), buf(10, rows_m, width),
        buf(4, rows_m, width), buf(nx, 32, width), buf(nx, 32, width),
        buf(ny, 16, width), buf(ny, 16, width),
        pltpu.VMEM((ny, 8, 128), F32), pltpu.VMEM((ny, 8, 128), F32),
        pltpu.VMEM((8, 128), F32), pltpu.VMEM((8, 128), F32),
        dma((5,)), dma((2,)), dma((3,)), dma((2, ny)), dma((2, ny)), dma((ny,)), dma((ny,)),
        dma((2, nx)), dma((2, nx)), dma((2, 3)), dma((2, 16)), dma((2, 16)), dma((2, 16)), dma((2, 16)), dma((2, 16)),
        dma((2,)), dma((2,)),
        dma((2, 10)), dma((2, 10)), dma((2, 10)), dma((2, 10)), dma((2, 16)), dma((2, 4)),
        dma((2, nx)), dma((2, nx)), dma((2, ny)), dma((2, ny)), dma((ny,)), dma((ny,)), dma((1,)), dma((1,)),
    ]
    rows, scores = pl.pallas_call(
        functools.partial(kernel, ny, nx, 4 * nx),
        out_shape=(
            jax.ShapeDtypeStruct((tokens.shape[0], depth), BF16),
            jax.ShapeDtypeStruct((tokens.shape[0], expert_ids.shape[1] // 2), F32),
        ),
        in_specs=[hbm] * 8,
        out_specs=(hbm, hbm),
        scratch_shapes=scratch,
        compiler_params=pltpu.CompilerParams(
            collective_id=0, has_side_effects=True, vmem_limit_bytes=60 * 1024 * 1024
        ),
    )(tokens, cotangent, group_ids, expert_ids, gate_weights, w_gate, w_up, w_down)
    return rows[:, :depth // 2], rows[:, depth // 2:], scores


def solution(mesh):
    rows = P(("group", "expert"), None)
    return jax.shard_map(
        body,
        mesh=mesh,
        in_specs=(
            rows, rows, rows, rows, rows,
            P(("group", "expert"), None, "ffn"),
            P(("group", "expert"), None, "ffn"),
            P(("group", "expert"), "ffn", None),
        ),
        out_specs=(
            P(("group", "expert"), "ffn"),
            P(("group", "expert"), "ffn"),
            P(("group", "expert"), "ffn"),
        ),
        check_vma=False,
    )
```
